256 devices in a mesh: seq: 32 (over y, z), head: 8 (over x, core).
Axes of the slice: x: 4, y: 4, z: 8, core: 2. Of those that a mesh axis runs over, the one named last changes fastest.
Arguments:
- queries: bfloat16 [16384, 8192], P('seq', 'head'), may hold values from -6 to 6
- keys: bfloat16 [16384, 8192], P('seq', 'head'), may hold values from -6 to 6
- values: bfloat16 [16384, 8192], P('seq', 'head'), may hold values from -6 to 6
- log_decay: float32 [16384, 64], P('seq', 'head'), may hold values from -1.55 to 0, as said below
- gate: bfloat16 [16384, 8192], P('seq', 'head'), may hold values from -6 to 6
- norm_gain: float32 [8192], P('head'), may hold values from 0.1 to 1.9
- w_out: bfloat16 [8192, 3072], P('head'), may hold values from -0.09375 to 0.09375
Outputs:
- output: bfloat16 [16384, 3072], P('seq', 'head')
The draws below stay inside these ranges and needn't reach their ends.
Inputs may be any that keep to these rules, and one draw needn't show every extreme that they name: log_decay is negative.
All inputs are finite; a program needn't handle non-finite values.
Results may differ from the reference program's by a relative error of at most 0.024.
Values may be sent and summed in bfloat16 or wider, within the bound.
A program may use at most 128 MiB of HBM per device.

```python
import math
import jax
import jax.numpy as jnp
from jax import lax

HEAD_TOTAL = 64
HD = 128
D = 3072
BLOCK = 256
TOKEN_TOTAL = 16384
N_HEAD = 8


def draw_log_decay(key, part):
    key = jax.random.fold_in(key, 11)
    key_fast, key_slow, key_factor, key_position, key_length = jax.random.split(key, 5)
    fast_share = 0.5
    fast_heads = jax.random.uniform(key_fast, (HEAD_TOTAL,)) < fast_share
    slow_rate = jax.random.uniform(key_slow, (HEAD_TOTAL,), minval=0.2, maxval=0.6) / TOKEN_TOTAL
    fast_rate = 1.0 / min(40, BLOCK // 4)
    baseline_decay_rate = jnp.where(fast_heads, fast_rate, slow_rate)
    decay_factor = jnp.exp(jax.random.uniform(key_factor, (TOKEN_TOTAL, HEAD_TOTAL), minval=-math.log(2.0), maxval=math.log(2.0)))
    segment_position = jax.random.randint(key_position, (3,), 0, TOKEN_TOTAL)
    segment_length = jax.random.uniform(key_length, (3, HEAD_TOTAL), minval=0.22, maxval=0.5)
    token_positions = jnp.arange(TOKEN_TOTAL)
    token_segments = jnp.zeros((TOKEN_TOTAL, HEAD_TOTAL), jnp.float32)
    for token_segment in range(3):
        token_segments = token_segments + jnp.where((token_positions == segment_position[token_segment])[:, None], segment_length[token_segment][None, :], 0.0)
    return (-(baseline_decay_rate[None, :] * decay_factor + token_segments)).astype(jnp.float32)


def raised(values, own_key, source, target, parts, factor):
    def block_of(axis_at):
        return (jnp.arange(values.shape[axis_at]) // (values.shape[axis_at] // parts)).reshape((-1,) + (1,) * (values.ndim - 1 - axis_at))

    near = jax.random.permutation(own_key, parts)[block_of(target)]
    other_side = (block_of(target) + parts // 2) % parts
    return jnp.where((block_of(source) == near) | (block_of(source) == other_side), factor * values, values)


def block_scale(stream_key, extent, cuts, low, high):
    gain = 1.0
    for position, parts in cuts:
        draws = jax.random.uniform(jax.random.fold_in(jax.random.fold_in(stream_key, 6), position), (parts,), jnp.float32, low / len(cuts), high / len(cuts))
        gain = gain * jnp.repeat(jnp.exp(draws), extent[position] // parts).reshape((-1,) + (1,) * (len(extent) - 1 - position))
    return gain


def centred(rng, extent, spread, limit, cuts=(), held_as=jnp.bfloat16):
    factor_of = block_scale(rng, extent, cuts, -0.22, 0.18) if cuts else 1.0
    drawn = jax.random.normal(rng, extent, jnp.float32) * spread * factor_of
    return jnp.minimum(jnp.maximum(drawn, -limit), limit).astype(held_as)


def noise_with(key, dims, width, most, pieces, heavy, kind=jnp.bfloat16):
    array = width * jax.random.normal(key, dims, jnp.float32)
    if pieces:
        array = array * block_scale(key, dims, pieces, -0.22, 0.18)
    return jnp.clip(raised(array, jax.random.fold_in(key, 3), *heavy), -most, most).astype(kind)


def setup_inputs(seed: int = 0) -> dict:
    seeds = jax.random.split(jax.random.key(seed), 8)
    return {
        "queries": centred(seeds[0], (TOKEN_TOTAL, HEAD_TOTAL * HD), 1.0, 6.0, ((0, 32), (1, 8))),
        "keys": centred(seeds[1], (TOKEN_TOTAL, HEAD_TOTAL * HD), 1.0, 6.0, ((0, 32), (1, 8))),
        "values": centred(seeds[2], (TOKEN_TOTAL, HEAD_TOTAL * HD), 1.0, 6.0, ((0, 32), (1, 8))),
        "log_decay": draw_log_decay(jax.random.fold_in(seeds[7], 71), 0),
        "gate": centred(seeds[4], (TOKEN_TOTAL, HEAD_TOTAL * HD), 1.5, 6.0, ((0, 32), (1, 8))),
        "norm_gain": jnp.clip(1.0 + 0.18 * jax.random.normal(seeds[5], (HEAD_TOTAL * HD,), jnp.float32), 0.1, 1.9),
        "w_out": noise_with(seeds[6], (HEAD_TOTAL * HD, D), (HEAD_TOTAL * HD) ** -0.5, 0.09375, ((0, 8),), (0, 1, 8, 2.0)),
    }


def rounded(value):
    return lax.optimization_barrier(value.astype(jnp.bfloat16)).astype(jnp.float32)

def reference(queries, keys, values, log_decay, gate, norm_gain, w_out):
    block_count = TOKEN_TOTAL // BLOCK
    block_shape = (block_count, BLOCK, HEAD_TOTAL, HD)
    query_blocks = queries.reshape(block_shape)
    key_blocks = keys.reshape(block_shape)
    value_blocks = values.reshape(block_shape)
    decay_blocks = log_decay.reshape(block_count, BLOCK, HEAD_TOTAL)
    causal = jnp.tril(jnp.ones((BLOCK, BLOCK), dtype=bool))

    def block_step(carry_state, block_item):
        query_here, key_here, value_here, decay_here = block_item
        cumulative = jnp.cumsum(decay_here, axis=0)
        block_total = cumulative[-1]
        query_float = query_here.astype(jnp.float32)
        key_float = key_here.astype(jnp.float32)
        value_float = value_here.astype(jnp.float32)
        weighted_keys = rounded(key_float * jnp.exp(block_total[None, :] - cumulative)[:, :, None])
        state_half = rounded(carry_state)
        query_scaled = rounded(query_float * jnp.exp(cumulative)[:, :, None])
        inter_part = jnp.einsum('ihd,hde->ihe', query_scaled, state_half)
        scores = jnp.einsum('ihd,jhd->hij', query_float, key_float)
        cum_heads = jnp.swapaxes(cumulative, 0, 1)
        between = cum_heads[:, :, None] - cum_heads[:, None, :]
        weights = jnp.where(causal[None], jnp.exp(jnp.minimum(between, 0.0)), 0.0)
        scores_half = rounded(scores * weights)
        intra_part = jnp.einsum('hij,jhe->ihe', scores_half, value_float)
        new_state = jnp.exp(block_total)[:, None, None] * carry_state + jnp.einsum('thd,the->hde', weighted_keys, value_float)
        return (new_state, intra_part + inter_part)
    _, attended = lax.scan(block_step, jnp.zeros((HEAD_TOTAL, HD, HD), jnp.float32), (query_blocks, key_blocks, value_blocks, decay_blocks))
    attended = attended.reshape(TOKEN_TOTAL, HEAD_TOTAL, HD)
    normed = attended * lax.rsqrt(lax.optimization_barrier(jnp.mean(attended * attended, axis=-1, keepdims=True)) + 1e-06) * norm_gain.reshape(HEAD_TOTAL, HD)
    hidden = (normed.reshape(TOKEN_TOTAL, HEAD_TOTAL * HD) * jax.nn.sigmoid(gate.astype(jnp.float32))).astype(jnp.bfloat16)
    group_width = HEAD_TOTAL * HD // N_HEAD

    def add_group(running, group):
        start = group * group_width
        group_part = jnp.dot(lax.dynamic_slice_in_dim(hidden, start, group_width, 1), lax.dynamic_slice_in_dim(w_out, start, group_width, 0), preferred_element_type=jnp.float32)
        return (running + rounded(group_part), None)
    total_out, _ = lax.scan(add_group, jnp.zeros((TOKEN_TOTAL, D), jnp.float32), jnp.arange(N_HEAD).astype(jnp.int32))
    return total_out.astype(jnp.bfloat16)
```

```python
import jax
import jax.numpy as jnp
from jax import lax
from jax.experimental import pallas as pl
from jax.experimental.pallas import tpu as pltpu
from jax.sharding import PartitionSpec as P

HD = 128
BLOCK = 256
NX, NY, NZ = 4, 4, 8
ROWS = 512
HEADS = 8
FEAT = HEADS * HD
CW = 384
TILE = 128
NT = ROWS // TILE
HALF = TILE // 2
EARLY = 4

F32, BF16 = jnp.float32, jnp.bfloat16
EXACT = lax.Precision.HIGHEST
MESH = pl.DeviceIdType.MESH


def remote(src, dst, send_sem, recv_sem, device_id):
    return pltpu.make_async_remote_copy(
        src_ref=src,
        dst_ref=dst,
        send_sem=send_sem,
        recv_sem=recv_sem,
        device_id=device_id,
        device_id_type=MESH,
    )


def columns(index, width=HD):
    return pl.ds(pl.multiple_of(index * width, HD), width)


def kernel(
    q_hbm, k_hbm, v_hbm, ld_hbm, gate_hbm, gain_hbm, w_hbm,
    out,
    q, k, v, ld, gate, gain, w_own, w_peer,
    cb, cumr, att, qs, gg, h_own, h_peer,
    lt, ltb, s_end, s_first, s_in, w_pre, cl_pre, t_out, t_in, rd_out, rd_in, p_out, p_in,
    opp, side, held, fwd, mine, passing, fin,
    load_sem, lt_s, lt_r, s1, r1, t_s, t_r, rd_s, rd_r, s3, r3, w_s, w_r, h_s, h_r,
    m1_s, m1_r, m2_s, m2_r, m3_s, m3_r,
):
    head, seq = lax.axis_index("head"), lax.axis_index("seq")
    z, y = lax.rem(seq, NZ), lax.div(seq, NZ)
    row0 = seq - z
    core, x = lax.rem(head, 2), lax.div(head, 2)
    other = {"head": head + 1 - 2 * core}
    x_right, x_left, x_opp = lax.rem(x + 1, NX), lax.rem(x + 3, NX), lax.rem(x + 2, NX)
    right, left = {"head": x_right * 2 + core}, {"head": x_left * 2 + core}

    def along_z(off):
        return lax.rem(z + off, NZ)

    def along_y(off):
        return lax.rem(y + off, NY)

    loads = [
        pltpu.make_async_copy(src, dst, load_sem.at[i])
        for i, (src, dst) in enumerate(
            ((ld_hbm, ld), (k_hbm, k), (v_hbm, v), (q_hbm, q), (gate_hbm, gate), (gain_hbm, gain))
        )
    ]
    w_loads = [
        pltpu.make_async_copy(
            w_hbm.at[:, pl.ds(pl.multiple_of((2 * i + core) * CW, HD), CW)],
            w_own.at[i],
            load_sem.at[6 + i],
        )
        for i in range(NX)
    ]
    w_sends = [
        remote(
            w_hbm.at[:, pl.ds(pl.multiple_of((2 * i + 1 - core) * CW, HD), CW)],
            w_peer.at[i],
            w_s.at[i],
            w_r.at[i],
            other,
        )
        for i in range(NX)
    ]
    for copy in loads:
        copy.start()

    barrier = pltpu.get_barrier_semaphore()
    for off in range(1, NZ):
        pl.semaphore_signal(
            barrier, inc=1, device_id={"seq": row0 + along_z(off)}, device_id_type=MESH
        )
    for off in range(1, NY):
        pl.semaphore_signal(
            barrier, inc=1, device_id={"seq": along_y(off) * NZ + z}, device_id_type=MESH
        )
    for device in (other, right, left):
        pl.semaphore_signal(barrier, inc=1, device_id=device, device_id_type=MESH)

    at_row = lax.broadcasted_iota(jnp.int32, (BLOCK, BLOCK), 0)
    at_col = lax.broadcasted_iota(jnp.int32, (BLOCK, BLOCK), 1)
    lower = jnp.where(at_row >= at_col, 1.0, 0.0).astype(F32)
    upper = jnp.where(at_row <= at_col, 1.0, 0.0).astype(F32)
    loads[0].wait()
    for b in range(2):
        rows = slice(b * BLOCK, (b + 1) * BLOCK)
        decay = ld[rows, :]
        cum = jnp.dot(lower, decay, precision=EXACT, preferred_element_type=F32)
        cumr[:, rows] = lax.dot_general(
            decay, upper, (((0,), (0,)), ((), ())), precision=EXACT, preferred_element_type=F32
        )
        for h in range(HEADS):
            cb[rows, h * HD : (h + 1) * HD] = jnp.broadcast_to(cum[:, h : h + 1], (BLOCK, HD))
    lt[...] = jnp.broadcast_to(
        cumr[:, BLOCK - 1 : BLOCK] + cumr[:, ROWS - 1 : ROWS], (HEADS, HD)
    )
    ltb[z] = lt[...]
    pl.semaphore_wait(barrier, NZ - 1 + NY - 1 + 3)

    def lt_copy(off):
        return remote(
            lt, ltb.at[z], lt_s.at[off], lt_r.at[z], {"seq": row0 + along_z(off)}
        )

    for off in range(1, NZ):
        lt_copy(off).start()

    def state_copy(h):
        return remote(s_end.at[h], s_in.at[z], s1.at[h], r1.at[z], {"seq": row0 + h})

    loads[1].wait()
    loads[2].wait()

    @pl.loop(0, HEADS)
    def _(i):
        odd = lax.rem(i, 2)
        h = along_z(4 + lax.div(i + 1, 2) * (2 * odd - 1))
        hc = columns(h)
        parts = []
        for b in range(2):
            rows = slice(b * BLOCK, (b + 1) * BLOCK)
            total = cb[(b + 1) * BLOCK - 1 : (b + 1) * BLOCK, hc]
            weighted = (k[rows, hc].astype(F32) * jnp.exp(total - cb[rows, hc])).astype(BF16)
            parts.append(
                lax.dot_general(
                    weighted, v[rows, hc], (((0,), (0,)), ((), ())), preferred_element_type=F32
                )
            )
        s_first[h] = parts[0].astype(BF16)
        whole = (jnp.exp(cb[ROWS - 1 : ROWS, hc]) * parts[0] + parts[1]).astype(BF16)
        s_end[h] = whole

        @pl.when(i < HEADS - 1)
        def _():
            state_copy(h).start()

        @pl.when(i == HEADS - 1)
        def _():
            s_in[z] = whole

    for copy in w_sends:
        copy.start()
    for copy in w_loads:
        copy.start()
    for copy in loads[3:]:
        copy.wait()

    def within(h):
        hc = columns(h)
        for b in range(2):
            rows = slice(b * BLOCK, (b + 1) * BLOCK)
            query = q[rows, hc]
            scores = lax.dot_general(
                query, k[rows, hc], (((1,), (1,)), ((), ())), preferred_element_type=F32
            )
            col = cb[rows, hc]
            between = jnp.concatenate([col, col], axis=1) - cumr[pl.ds(h, 1), rows]
            weights = jnp.exp(jnp.where(at_row >= at_col, jnp.minimum(between, 0.0), -1e30))
            attended = jnp.dot(
                (scores * weights).astype(BF16), v[rows, hc], preferred_element_type=F32
            )
            scaled = query.astype(F32) * jnp.exp(col)
            if b == 1:
                attended += jnp.dot(
                    scaled.astype(BF16), s_first[h], preferred_element_type=F32
                )
                scaled = query.astype(F32) * jnp.exp(col + cb[BLOCK - 1 : BLOCK, hc])
            qs[rows, hc] = scaled.astype(BF16)
            att[rows, hc] = attended
            gg[rows, hc] = gain[pl.ds(h, 1), :] * jax.nn.sigmoid(gate[rows, hc].astype(F32))

    @pl.loop(0, EARLY)
    def _(h):
        within(h)

    for off in range(1, NZ):
        there = along_z(off)
        remote(lt, ltb.at[there], lt_s.at[off], lt_r.at[there], other).wait_recv()
        remote(s_end.at[0], s_in.at[there], s1.at[0], r1.at[there], other).wait_recv()
    state = jnp.zeros((HD, HD), F32)
    log = jnp.zeros((1, HD), F32)
    for there in range(NZ):
        w_pre[there] = state
        cl_pre[there : there + 1, :] = log
        step = ltb[there, pl.ds(z, 1), :]
        state = jnp.exp(step) * state + s_in[there].astype(F32)
        log = log + step
    t_out[...] = state.astype(BF16)
    rd_out[...] = jnp.broadcast_to(log, (8, HD))
    t_in[y] = t_out[...]
    rd_in[y] = rd_out[...]

    def row_copies(off):
        device = {"seq": along_y(off) * NZ + z}
        return (
            remote(t_out, t_in.at[y], t_s.at[off], t_r.at[y], device),
            remote(rd_out, rd_in.at[y], rd_s.at[off], rd_r.at[y], device),
        )

    for off in range(1, NY):
        for copy in row_copies(off):
            copy.start()
    for off in range(1, NY):
        there = along_y(off)
        remote(t_out, t_in.at[there], t_s.at[off], t_r.at[there], other).wait_recv()
        remote(rd_out, rd_in.at[there], rd_s.at[off], rd_r.at[there], other).wait_recv()
    before = jnp.zeros((HD, HD), F32)
    for there in range(NY - 1):
        joined = jnp.exp(rd_in[there][0:1, :]) * before + t_in[there].astype(F32)
        before = jnp.where(there < y, joined, before)

    def prefix_copy(there):
        return remote(
            p_out.at[there], p_in.at[z], s3.at[there], r3.at[z], {"seq": row0 + there}
        )

    for off in (4, 5, 3, 6, 2, 7, 1, 0):
        there = along_z(off)
        entering = (
            jnp.exp(cl_pre[pl.ds(there, 1), :]) * before + w_pre[there]
        ).astype(BF16)
        if off:
            p_out[there] = entering
            prefix_copy(there).start()
        else:
            p_in[z] = entering

    @pl.loop(EARLY, HEADS)
    def _(h):
        within(h)

    for copy in w_loads:
        copy.wait()
    for copy in w_sends:
        copy.wait_recv()
    for off in range(1, NZ):
        there = along_z(off)
        remote(p_out.at[0], p_in.at[there], s3.at[0], r3.at[there], other).wait_recv()

    def tile(t):
        return pl.ds(pl.multiple_of(t * TILE, TILE), TILE)

    def hidden_copy(t):
        return remote(h_own.at[tile(t)], h_peer.at[tile(t)], h_s.at[t], h_r.at[t], other)

    def make_hidden(t):
        rows = tile(t)
        for h in range(HEADS):
            hc = slice(h * HD, (h + 1) * HD)
            attended = att[rows, hc] + jnp.dot(
                qs[rows, hc], p_in[h], preferred_element_type=F32
            )
            square = jnp.mean(attended * attended, axis=1, keepdims=True)
            h_own[rows, hc] = (attended * lax.rsqrt(square + 1e-06) * gg[rows, hc]).astype(BF16)
        hidden_copy(t).start()

    def chunk(t, i):
        return jnp.dot(h_own[tile(t), :], w_own[i], preferred_element_type=F32) + jnp.dot(
            h_peer[tile(t), :], w_peer[i], preferred_element_type=F32
        )

    targets = (right, left)
    halves = (slice(0, HALF), slice(HALF, TILE))

    def first_copy(t, way):
        return remote(
            opp.at[t, way], fwd.at[way, t], m1_s.at[way, t], m1_r.at[way, t], targets[way]
        )

    def side_copy(t, way):
        return remote(
            side.at[way, t], fin.at[way, t, 1 - way], m2_s.at[way, t], m2_r.at[way, t], targets[way]
        )

    def passing_copy(t, way):
        return remote(
            passing.at[way, t], fin.at[way, t, way], m3_s.at[way, t], m3_r.at[way, t], targets[way]
        )

    def project(t):
        hidden_copy(t).wait_recv()
        far = chunk(t, x_opp).astype(BF16)
        for way in range(2):
            opp[t, way] = far[halves[way]]
            first_copy(t, way).start()
        for way, i in enumerate((x_right, x_left)):
            near = chunk(t, i)
            side[way, t] = near[halves[1 - way]].astype(BF16)
            side_copy(t, way).start()
            held[way, t] = near[halves[way]]
        mine[t] = chunk(t, x)

    def pass_on(t):
        for way in range(2):
            first_copy(t, way).wait_recv()
            passing[way, t] = (held[way, t] + fwd[way, t].astype(F32)).astype(BF16)
            passing_copy(t, way).start()

    make_hidden(0)

    @pl.loop(0, NT)
    def _(t):
        @pl.when(t < NT - 1)
        def _():
            make_hidden(t + 1)

        project(t)

        @pl.when(t > 0)
        def _():
            pass_on(t - 1)

    pass_on(NT - 1)

    @pl.loop(0, NT)
    def _(t):
        for way in range(2):
            side_copy(t, way).wait_recv()
            passing_copy(t, way).wait_recv()
        for half in range(2):
            rows = pl.ds(pl.multiple_of(t * TILE + half * HALF, HALF), HALF)
            out[rows, :] = (
                mine[t, halves[half]]
                + fin[0, t, half].astype(F32)
                + fin[1, t, half].astype(F32)
            ).astype(BF16)

    for off in range(1, NZ):
        lt_copy(off).wait_send()
        there = along_z(off)
        state_copy(there).wait_send()
        prefix_copy(there).wait_send()
    for off in range(1, NY):
        for copy in row_copies(off):
            copy.wait_send()
    for copy in w_sends:
        copy.wait_send()

    @pl.loop(0, NT)
    def _(t):
        hidden_copy(t).wait_send()
        for way in range(2):
            first_copy(t, way).wait_send()
            side_copy(t, way).wait_send()
            passing_copy(t, way).wait_send()


def per_device(queries, keys, values, log_decay, gate, norm_gain, w_out):
    vmem, dma = pltpu.VMEM, pltpu.SemaphoreType.DMA
    scratch = [
        vmem((ROWS, FEAT), BF16),
        vmem((ROWS, FEAT), BF16),
        vmem((ROWS, FEAT), BF16),
        vmem((ROWS, HEADS), F32),
        vmem((ROWS, FEAT), BF16),
        vmem((HEADS, HD), F32),
        vmem((NX, FEAT, CW), BF16),
        vmem((NX, FEAT, CW), BF16),
        vmem((ROWS, FEAT), F32),
        vmem((HEADS, ROWS), F32),
        vmem((ROWS, FEAT), F32),
        vmem((ROWS, FEAT), BF16),
        vmem((ROWS, FEAT), F32),
        vmem((ROWS, FEAT), BF16),
        vmem((ROWS, FEAT), BF16),
        vmem((HEADS, HD), F32),
        vmem((NZ, HEADS, HD), F32),
        vmem((HEADS, HD, HD), BF16),
        vmem((HEADS, HD, HD), BF16),
        vmem((NZ, HD, HD), BF16),
        vmem((NZ, HD, HD), F32),
        vmem((NZ, HD), F32),
        vmem((HD, HD), BF16),
        vmem((NY, HD, HD), BF16),
        vmem((8, HD), F32),
        vmem((NY, 8, HD), F32),
        vmem((NZ, HD, HD), BF16),
        vmem((HEADS, HD, HD), BF16),
        vmem((NT, 2, HALF, CW), BF16),
        vmem((2, NT, HALF, CW), BF16),
        vmem((2, NT, HALF, CW), F32),
        vmem((2, NT, HALF, CW), BF16),
        vmem((NT, TILE, CW), F32),
        vmem((2, NT, HALF, CW), BF16),
        vmem((2, NT, 2, HALF, CW), BF16),
        dma((6 + NX,)),
        dma((NZ,)), dma((NZ,)),
        dma((NZ,)), dma((NZ,)),
        dma((NY,)), dma((NY,)),
        dma((NY,)), dma((NY,)),
        dma((NZ,)), dma((NZ,)),
        dma((NX,)), dma((NX,)),
        dma((NT,)), dma((NT,)),
        dma((2, NT)), dma((2, NT)),
        dma((2, NT)), dma((2, NT)),
        dma((2, NT)), dma((2, NT)),
    ]
    return pl.pallas_call(
        kernel,
        out_shape=jax.ShapeDtypeStruct((ROWS, CW), BF16),
        in_specs=[pl.BlockSpec(memory_space=pl.ANY)] * 7,
        out_specs=pl.BlockSpec(memory_space=pltpu.VMEM),
        scratch_shapes=scratch,
        compiler_params=pltpu.CompilerParams(
            collective_id=0, has_side_effects=True, vmem_limit_bytes=56 * 1024 * 1024
        ),
        cost_estimate=pl.CostEstimate(
            flops=2 * ROWS * FEAT * (3072 + 2 * BLOCK + 2 * HD),
            bytes_accessed=11_000_000,
            transcendentals=ROWS * FEAT * 4,
        ),
    )(queries, keys, values, log_decay, gate, norm_gain.reshape(HEADS, HD), w_out)


def solution(mesh):
    placed = (
        P("seq", "head"),
        P("seq", "head"),
        P("seq", "head"),
        P("seq", "head"),
        P("seq", "head"),
        P("head"),
        P("head", None),
    )
    return jax.shard_map(
        per_device, mesh=mesh, in_specs=placed, out_specs=P("seq", "head"), check_vma=False
    )
```

```python
import jax
import jax.numpy as jnp
from jax import lax
from jax.experimental import pallas as pl
from jax.experimental.pallas import tpu as pltpu
from jax.sharding import PartitionSpec as P

HD = 128
BLOCK = 256
NX, NY, NZ = 4, 4, 8
ROWS = 512
HEADS = 8
FEAT = HEADS * HD
CW = 384
TILE = 128
NT = ROWS // TILE
HALF = TILE // 2
EARLY = 6

F32, BF16 = jnp.float32, jnp.bfloat16
EXACT = lax.Precision.HIGHEST
MESH = pl.DeviceIdType.MESH


def remote(src, dst, send_sem, recv_sem, device_id):
    return pltpu.make_async_remote_copy(
        src_ref=src,
        dst_ref=dst,
        send_sem=send_sem,
        recv_sem=recv_sem,
        device_id=device_id,
        device_id_type=MESH,
    )


def columns(index, width=HD):
    return pl.ds(pl.multiple_of(index * width, HD), width)


def kernel(
    q_hbm, k_hbm, v_hbm, ld_hbm, gate_hbm, gain_hbm, w_hbm,
    out,
    q, k, v, ld, gate, gain, w_own, w_peer,
    cb, cumr, att, qs, gg, h_own, h_peer,
    lt, ltb, s_end, s_first, s_in, w_pre, cl_pre, t_out, t_in, rd_out, rd_in, rows_before, p_out, p_in,
    opp, side, held, fwd, mine, passing, fin,
    load_sem, lt_s, lt_r, s1, r1, t_s, t_r, rd_s, rd_r, s3, r3, w_s, w_r, h_s, h_r,
    m1_s, m1_r, m2_s, m2_r, m3_s, m3_r,
):
    head, seq = lax.axis_index("head"), lax.axis_index("seq")
    z, y = lax.rem(seq, NZ), lax.div(seq, NZ)
    row0 = seq - z
    core, x = lax.rem(head, 2), lax.div(head, 2)
    other = {"head": head + 1 - 2 * core}
    x_right, x_left, x_opp = lax.rem(x + 1, NX), lax.rem(x + 3, NX), lax.rem(x + 2, NX)
    right, left = {"head": x_right * 2 + core}, {"head": x_left * 2 + core}

    def along_z(off):
        return lax.rem(z + off, NZ)

    def along_y(off):
        return lax.rem(y + off, NY)

    loads = [
        pltpu.make_async_copy(src, dst, load_sem.at[i])
        for i, (src, dst) in enumerate(
            ((ld_hbm, ld), (k_hbm, k), (v_hbm, v), (q_hbm, q), (gate_hbm, gate), (gain_hbm, gain))
        )
    ]
    w_loads = [
        pltpu.make_async_copy(
            w_hbm.at[:, pl.ds(pl.multiple_of((2 * i + core) * CW, HD), CW)],
            w_own.at[i],
            load_sem.at[6 + i],
        )
        for i in range(NX)
    ]
    w_sends = [
        remote(
            w_hbm.at[:, pl.ds(pl.multiple_of((2 * i + 1 - core) * CW, HD), CW)],
            w_peer.at[i],
            w_s.at[i],
            w_r.at[i],
            other,
        )
        for i in range(NX)
    ]
    for copy in loads:
        copy.start()

    barrier = pltpu.get_barrier_semaphore()
    for off in range(1, NZ):
        pl.semaphore_signal(
            barrier, inc=1, device_id={"seq": row0 + along_z(off)}, device_id_type=MESH
        )
    for off in range(1, NY):
        pl.semaphore_signal(
            barrier, inc=1, device_id={"seq": along_y(off) * NZ + z}, device_id_type=MESH
        )
    for device in (other, right, left):
        pl.semaphore_signal(barrier, inc=1, device_id=device, device_id_type=MESH)

    at_row = lax.broadcasted_iota(jnp.int32, (BLOCK, BLOCK), 0)
    at_col = lax.broadcasted_iota(jnp.int32, (BLOCK, BLOCK), 1)
    lower = jnp.where(at_row >= at_col, 1.0, 0.0).astype(F32)
    upper = jnp.where(at_row <= at_col, 1.0, 0.0).astype(F32)
    loads[0].wait()
    for b in range(2):
        rows = slice(b * BLOCK, (b + 1) * BLOCK)
        decay = ld[:, rows]
        cum = lax.dot_general(
            lower, decay, (((1,), (1,)), ((), ())), precision=EXACT, preferred_element_type=F32
        )
        cumr[:, rows] = jnp.dot(decay, upper, precision=EXACT, preferred_element_type=F32)
        for h in range(HEADS):
            cb[rows, h * HD : (h + 1) * HD] = jnp.broadcast_to(cum[:, h : h + 1], (BLOCK, HD))
    lt[...] = jnp.broadcast_to(
        cumr[:, BLOCK - 1 : BLOCK] + cumr[:, ROWS - 1 : ROWS], (HEADS, HD)
    )
    ltb[z] = lt[...]

    def lt_copy(off):
        return remote(
            lt, ltb.at[z], lt_s.at[off], lt_r.at[z], {"seq": row0 + along_z(off)}
        )

    def state_copy(h):
        return remote(s_end.at[h], s_in.at[z], s1.at[h], r1.at[z], {"seq": row0 + h})

    def make_state(h):
        hc = columns(h)
        parts = []
        for b in range(2):
            rows = slice(b * BLOCK, (b + 1) * BLOCK)
            total = cb[(b + 1) * BLOCK - 1 : (b + 1) * BLOCK, hc]
            weighted = (k[rows, hc].astype(F32) * jnp.exp(total - cb[rows, hc])).astype(BF16)
            parts.append(
                lax.dot_general(
                    weighted, v[rows, hc], (((0,), (0,)), ((), ())), preferred_element_type=F32
                )
            )
        s_first[h] = parts[0].astype(BF16)
        s_end[h] = (jnp.exp(cb[ROWS - 1 : ROWS, hc]) * parts[0] + parts[1]).astype(BF16)

    def far_first(i):
        return along_z(4 + lax.div(i + 1, 2) * (2 * lax.rem(i, 2) - 1))

    ready = jnp.where(z < NZ // 2, HEADS - 1, 1)
    loads[1].wait()
    loads[2].wait()

    @pl.loop(0, HEADS)
    def _(i):
        make_state(far_first(i))

        @pl.when(i == ready)
        def _():
            pl.semaphore_wait(barrier, NZ - 1 + NY - 1 + 3)
            for off in range(1, NZ):
                lt_copy(off).start()

        @pl.when(i >= ready)
        def _():
            @pl.loop(jnp.where(i == ready, 0, i), jnp.minimum(i + 1, HEADS - 1))
            def _(j):
                state_copy(far_first(j)).start()

    s_in[z] = s_end[z]
    for copy in w_sends:
        copy.start()
    for copy in w_loads:
        copy.start()
    for copy in loads[3:]:
        copy.wait()

    def within(h):
        hc = columns(h)
        for b in range(2):
            rows = slice(b * BLOCK, (b + 1) * BLOCK)
            query = q[rows, hc]
            scores = lax.dot_general(
                query, k[rows, hc], (((1,), (1,)), ((), ())), preferred_element_type=F32
            )
            col = cb[rows, hc]
            between = jnp.concatenate([col, col], axis=1) - cumr[pl.ds(h, 1), rows]
            weights = jnp.exp(jnp.where(at_row >= at_col, jnp.minimum(between, 0.0), -1e30))
            attended = jnp.dot(
                (scores * weights).astype(BF16), v[rows, hc], preferred_element_type=F32
            )
            scaled = query.astype(F32) * jnp.exp(col)
            if b == 1:
                attended += jnp.dot(
                    scaled.astype(BF16), s_first[h], preferred_element_type=F32
                )
                scaled = query.astype(F32) * jnp.exp(col + cb[BLOCK - 1 : BLOCK, hc])
            qs[rows, hc] = scaled.astype(BF16)
            att[rows, hc] = attended
            gg[rows, hc] = gain[pl.ds(h, 1), :] * jax.nn.sigmoid(gate[rows, hc].astype(F32))

    @pl.loop(0, EARLY)
    def _(h):
        within(h)

    state = jnp.zeros((HD, HD), F32)
    log = jnp.zeros((1, HD), F32)
    for there in range(NZ):
        w_pre[there] = state
        cl_pre[there : there + 1, :] = log

        @pl.when(there != z)
        def _():
            remote(lt, ltb.at[there], lt_s.at[0], lt_r.at[there], other).wait_recv()
            remote(s_end.at[0], s_in.at[there], s1.at[0], r1.at[there], other).wait_recv()

        step = ltb[there, pl.ds(z, 1), :]
        state = jnp.exp(step) * state + s_in[there].astype(F32)
        log = log + step
    t_out[...] = state.astype(BF16)
    rd_out[...] = jnp.broadcast_to(log, (8, HD))

    def row_copies(there):
        device = {"seq": there * NZ + z}
        return (
            remote(t_out, t_in.at[y], t_s.at[there], t_r.at[y], device),
            remote(rd_out, rd_in.at[y], rd_s.at[there], rd_r.at[y], device),
        )

    for there in range(1, NY):

        @pl.when(there > y)
        def _():
            for copy in row_copies(there):
                copy.start()

    rows_before[...] = jnp.zeros((HD, HD), F32)
    for there in range(NY - 1):

        @pl.when(there < y)
        def _():
            remote(t_out, t_in.at[there], t_s.at[0], t_r.at[there], other).wait_recv()
            remote(rd_out, rd_in.at[there], rd_s.at[0], rd_r.at[there], other).wait_recv()
            rows_before[...] = jnp.exp(rd_in[there][0:1, :]) * rows_before[...] + t_in[
                there
            ].astype(F32)

    before = rows_before[...]

    def prefix_copy(there):
        return remote(
            p_out.at[there], p_in.at[z], s3.at[there], r3.at[z], {"seq": row0 + there}
        )

    for there in range(NZ):
        entering = (jnp.exp(cl_pre[there : there + 1, :]) * before + w_pre[there]).astype(BF16)
        p_out[there] = entering

        @pl.when(there != z)
        def _():
            prefix_copy(there).start()

    p_in[z] = p_out[z]

    @pl.loop(EARLY, HEADS)
    def _(h):
        within(h)

    for copy in w_loads:
        copy.wait()
    for copy in w_sends:
        copy.wait_recv()
    for off in range(1, NZ):
        there = along_z(off)
        remote(p_out.at[0], p_in.at[there], s3.at[0], r3.at[there], other).wait_recv()

    def tile(t):
        return pl.ds(pl.multiple_of(t * TILE, TILE), TILE)

    def hidden_copy(t):
        return remote(h_own.at[tile(t)], h_peer.at[tile(t)], h_s.at[t], h_r.at[t], other)

    def make_hidden(t):
        rows = tile(t)
        for h in range(HEADS):
            hc = slice(h * HD, (h + 1) * HD)
            attended = att[rows, hc] + jnp.dot(
                qs[rows, hc], p_in[h], preferred_element_type=F32
            )
            square = jnp.mean(attended * attended, axis=1, keepdims=True)
            h_own[rows, hc] = (attended * lax.rsqrt(square + 1e-06) * gg[rows, hc]).astype(BF16)
        hidden_copy(t).start()

    def chunk(t, i):
        return jnp.dot(h_own[tile(t), :], w_own[i], preferred_element_type=F32) + jnp.dot(
            h_peer[tile(t), :], w_peer[i], preferred_element_type=F32
        )

    targets = (right, left)
    halves = (slice(0, HALF), slice(HALF, TILE))

    def first_copy(t, way):
        return remote(
            opp.at[t, way], fwd.at[way, t], m1_s.at[way, t], m1_r.at[way, t], targets[way]
        )

    def side_copy(t, way):
        return remote(
            side.at[way, t], fin.at[way, t, 1 - way], m2_s.at[way, t], m2_r.at[way, t], targets[way]
        )

    def passing_copy(t, way):
        return remote(
            passing.at[way, t], fin.at[way, t, way], m3_s.at[way, t], m3_r.at[way, t], targets[way]
        )

    def send_far(t):
        hidden_copy(t).wait_recv()
        far = chunk(t, x_opp).astype(BF16)
        for way in range(2):
            opp[t, way] = far[halves[way]]
            first_copy(t, way).start()

    def send_near(t):
        for way, i in enumerate((x_right, x_left)):
            near = chunk(t, i)
            side[way, t] = near[halves[1 - way]].astype(BF16)
            side_copy(t, way).start()
            held[way, t] = near[halves[way]]

    def pass_on(t):
        for way in range(2):
            first_copy(t, way).wait_recv()
            passing[way, t] = (held[way, t] + fwd[way, t].astype(F32)).astype(BF16)
            passing_copy(t, way).start()

    make_hidden(0)

    @pl.loop(0, NT)
    def _(t):
        @pl.when(t < NT - 1)
        def _():
            make_hidden(t + 1)

        send_far(t)

    @pl.loop(0, NT)
    def _(t):
        send_near(t)

        @pl.when(t > 0)
        def _():
            pass_on(t - 1)

    @pl.loop(0, NT)
    def _(t):
        mine[t] = chunk(t, x)

    pass_on(NT - 1)

    @pl.loop(0, NT)
    def _(t):
        for way in range(2):
            side_copy(t, way).wait_recv()
            passing_copy(t, way).wait_recv()
        for half in range(2):
            rows = pl.ds(pl.multiple_of(t * TILE + half * HALF, HALF), HALF)
            out[rows, :] = (
                mine[t, halves[half]]
                + fin[0, t, half].astype(F32)
                + fin[1, t, half].astype(F32)
            ).astype(BF16)

    for off in range(1, NZ):
        lt_copy(off).wait_send()
        there = along_z(off)
        state_copy(there).wait_send()
        prefix_copy(there).wait_send()
    for there in range(1, NY):

        @pl.when(there > y)
        def _():
            for copy in row_copies(there):
                copy.wait_send()

    for copy in w_sends:
        copy.wait_send()

    @pl.loop(0, NT)
    def _(t):
        hidden_copy(t).wait_send()
        for way in range(2):
            first_copy(t, way).wait_send()
            side_copy(t, way).wait_send()
            passing_copy(t, way).wait_send()


def per_device(queries, keys, values, log_decay, gate, norm_gain, w_out):
    vmem, dma = pltpu.VMEM, pltpu.SemaphoreType.DMA
    scratch = [
        vmem((ROWS, FEAT), BF16),
        vmem((ROWS, FEAT), BF16),
        vmem((ROWS, FEAT), BF16),
        vmem((HEADS, ROWS), F32),
        vmem((ROWS, FEAT), BF16),
        vmem((HEADS, HD), F32),
        vmem((NX, FEAT, CW), BF16),
        vmem((NX, FEAT, CW), BF16),
        vmem((ROWS, FEAT), F32),
        vmem((HEADS, ROWS), F32),
        vmem((ROWS, FEAT), F32),
        vmem((ROWS, FEAT), BF16),
        vmem((ROWS, FEAT), F32),
        vmem((ROWS, FEAT), BF16),
        vmem((ROWS, FEAT), BF16),
        vmem((HEADS, HD), F32),
        vmem((NZ, HEADS, HD), F32),
        vmem((HEADS, HD, HD), BF16),
        vmem((HEADS, HD, HD), BF16),
        vmem((NZ, HD, HD), BF16),
        vmem((NZ, HD, HD), F32),
        vmem((NZ, HD), F32),
        vmem((HD, HD), BF16),
        vmem((NY, HD, HD), BF16),
        vmem((8, HD), F32),
        vmem((NY, 8, HD), F32),
        vmem((HD, HD), F32),
        vmem((NZ, HD, HD), BF16),
        vmem((HEADS, HD, HD), BF16),
        vmem((NT, 2, HALF, CW), BF16),
        vmem((2, NT, HALF, CW), BF16),
        vmem((2, NT, HALF, CW), F32),
        vmem((2, NT, HALF, CW), BF16),
        vmem((NT, TILE, CW), F32),
        vmem((2, NT, HALF, CW), BF16),
        vmem((2, NT, 2, HALF, CW), BF16),
        dma((6 + NX,)),
        dma((NZ,)), dma((NZ,)),
        dma((NZ,)), dma((NZ,)),
        dma((NY,)), dma((NY,)),
        dma((NY,)), dma((NY,)),
        dma((NZ,)), dma((NZ,)),
        dma((NX,)), dma((NX,)),
        dma((NT,)), dma((NT,)),
        dma((2, NT)), dma((2, NT)),
        dma((2, NT)), dma((2, NT)),
        dma((2, NT)), dma((2, NT)),
    ]
    return pl.pallas_call(
        kernel,
        out_shape=pltpu.VMEM((ROWS, CW), BF16),
        in_specs=[pl.BlockSpec(memory_space=pl.ANY)] * 7,
        out_specs=pl.BlockSpec(memory_space=pltpu.VMEM),
        scratch_shapes=scratch,
        compiler_params=pltpu.CompilerParams(
            collective_id=0, has_side_effects=True, vmem_limit_bytes=56 * 1024 * 1024
        ),
        cost_estimate=pl.CostEstimate(
            flops=2 * ROWS * FEAT * (3072 + 2 * BLOCK + 2 * HD),
            bytes_accessed=11_000_000,
            transcendentals=ROWS * FEAT * 4,
        ),
    )(queries, keys, values, log_decay.T, gate, norm_gain.reshape(HEADS, HD), w_out)


def solution(mesh):
    placed = (
        P("seq", "head"),
        P("seq", "head"),
        P("seq", "head"),
        P("seq", "head"),
        P("seq", "head"),
        P("head"),
        P("head", None),
    )
    return jax.shard_map(
        per_device, mesh=mesh, in_specs=placed, out_specs=P("seq", "head"), check_vma=False
    )
```

```python
import jax
import jax.numpy as jnp
from jax import lax
from jax.experimental import pallas as pl
from jax.experimental.pallas import tpu as pltpu
from jax.sharding import PartitionSpec as P

HD = 128
BLOCK = 256
NX, NY, NZ = 4, 4, 8
ROWS = 512
HEADS = 8
FEAT = HEADS * HD
CW = 384
TILE = 128
NT = ROWS // TILE
PARTS = 2
PD = HD // PARTS
FAR_FIRST = (4, 5, 3, 6, 2, 7, 1)
HALF = TILE // 2
EARLY = 6

F32, BF16 = jnp.float32, jnp.bfloat16
EXACT = lax.Precision.HIGHEST
MESH = pl.DeviceIdType.MESH


def remote(src, dst, send_sem, recv_sem, device_id):
    return pltpu.make_async_remote_copy(
        src_ref=src,
        dst_ref=dst,
        send_sem=send_sem,
        recv_sem=recv_sem,
        device_id=device_id,
        device_id_type=MESH,
    )


def columns(index, width=HD):
    return pl.ds(pl.multiple_of(index * width, HD), width)


def kernel(
    q_hbm, k_hbm, v_hbm, ld_hbm, gate_hbm, gain_hbm, w_hbm,
    out,
    q, k, v, ld, gate, gain, w_own, w_peer,
    cb, cumr, att, qs, gg, h_own, h_peer,
    lt, ltb, s_end, s_first, s_in, w_pre, cl_pre, t_out, t_in, rd_out, rd_in, rows_before, p_out, p_in,
    opp, side, held, fwd, mine, passing, fin,
    load_sem, lt_s, lt_r, s1, r1, t_s, t_r, rd_s, rd_r, s3, r3, w_s, w_r, h_s, h_r,
    m1_s, m1_r, m2_s, m2_r, m3_s, m3_r, ready_y, ready_x, ready_core,
):
    head, seq = lax.axis_index("head"), lax.axis_index("seq")
    z, y = lax.rem(seq, NZ), lax.div(seq, NZ)
    row0 = seq - z
    core, x = lax.rem(head, 2), lax.div(head, 2)
    other = {"head": head + 1 - 2 * core}
    x_right, x_left, x_opp = lax.rem(x + 1, NX), lax.rem(x + 3, NX), lax.rem(x + 2, NX)
    right, left = {"head": x_right * 2 + core}, {"head": x_left * 2 + core}

    def along_z(off):
        return lax.rem(z + off, NZ)

    def along_y(off):
        return lax.rem(y + off, NY)

    def load(i, src, dst):
        return pltpu.make_async_copy(src, dst, load_sem.at[i])

    ld_load = load(0, ld_hbm, ld)
    kv_loads = [load(1, k_hbm, k), load(2, v_hbm, v)]
    later_loads = [
        load(3, q_hbm, q),
        load(4, gate_hbm, gate),
        load(5, gain_hbm, gain),
    ]
    w_loads = [
        pltpu.make_async_copy(
            w_hbm.at[:, pl.ds(pl.multiple_of((2 * i + core) * CW, HD), CW)],
            w_own.at[i],
            load_sem.at[6 + i],
        )
        for i in range(NX)
    ]
    w_sends = [
        remote(
            w_hbm.at[:, pl.ds(pl.multiple_of((2 * i + 1 - core) * CW, HD), CW)],
            w_peer.at[i],
            w_s.at[i],
            w_r.at[i],
            other,
        )
        for i in range(NX)
    ]

    barrier = pltpu.get_barrier_semaphore()

    def greet(device):
        pl.semaphore_signal(barrier, inc=1, device_id=device, device_id_type=MESH)

    def answer(sem, device):
        pl.semaphore_signal(sem, inc=1, device_id=device, device_id_type=MESH)

    for off in FAR_FIRST:
        greet({"seq": row0 + along_z(off)})
    ld_load.start()
    for copy in kv_loads:
        copy.start()
    for there in range(1, NY):

        @pl.when(there > y)
        def _():
            greet({"seq": there * NZ + z})

    @pl.when(x_right > x)
    def _():
        greet(right)

    @pl.when(x_left > x)
    def _():
        greet(left)

    @pl.when(core == 0)
    def _():
        greet(other)

    greeted = NZ - 1 + y + core + jnp.where(x_right < x, 1, 0) + jnp.where(x_left < x, 1, 0)

    at_row = lax.broadcasted_iota(jnp.int32, (BLOCK, BLOCK), 0)
    at_col = lax.broadcasted_iota(jnp.int32, (BLOCK, BLOCK), 1)
    lower = jnp.where(at_row >= at_col, 1.0, 0.0).astype(F32)
    upper = jnp.where(at_row <= at_col, 1.0, 0.0).astype(F32)
    ld_load.wait()
    for b in range(2):
        rows = slice(b * BLOCK, (b + 1) * BLOCK)
        decay = ld[:, rows]
        cum = lax.dot_general(
            lower, decay, (((1,), (1,)), ((), ())), precision=EXACT, preferred_element_type=F32
        )
        cumr[:, rows] = jnp.dot(decay, upper, precision=EXACT, preferred_element_type=F32)
        for h in range(HEADS):
            cb[rows, h * HD : (h + 1) * HD] = jnp.broadcast_to(cum[:, h : h + 1], (BLOCK, HD))
    lt[...] = jnp.broadcast_to(
        cumr[:, BLOCK - 1 : BLOCK] + cumr[:, ROWS - 1 : ROWS], (HEADS, HD)
    )
    ltb[z] = lt[...]

    def lt_copy(off):
        return remote(
            lt, ltb.at[z], lt_s.at[off], lt_r.at[z], {"seq": row0 + along_z(off)}
        )

    def state_copy(part, h):
        return remote(
            s_end.at[part, h],
            s_in.at[part, z],
            s1.at[part, h],
            r1.at[part, z],
            {"seq": row0 + h},
        )

    for copy in kv_loads:
        copy.wait()
    for h in range(HEADS):
        hc = slice(h * HD, (h + 1) * HD)
        ends = []
        for b in range(2):
            rows = slice(b * BLOCK, (b + 1) * BLOCK)
            total = cb[(b + 1) * BLOCK - 1 : (b + 1) * BLOCK, hc]
            weighted = (k[rows, hc].astype(F32) * jnp.exp(total - cb[rows, hc])).astype(BF16)
            ends.append(
                lax.dot_general(
                    weighted, v[rows, hc], (((0,), (0,)), ((), ())), preferred_element_type=F32
                )
            )
        s_first[h] = ends[0].astype(BF16)
        whole = (jnp.exp(cb[ROWS - 1 : ROWS, hc]) * ends[0] + ends[1]).astype(BF16)
        for part in range(PARTS):
            s_end[part, h] = whole[part * PD : (part + 1) * PD]

    pl.semaphore_wait(barrier, greeted)
    for part in range(PARTS):
        for off in FAR_FIRST:
            state_copy(part, along_z(off)).start()
        if part == 0:
            for off in FAR_FIRST:
                lt_copy(off).start()
    for part in range(PARTS):
        s_in[part, z] = s_end[part, z]
    for there in range(NY - 1):

        @pl.when(there < y)
        def _():
            answer(ready_y.at[y], {"seq": there * NZ + z})

    @pl.when(x_right < x)
    def _():
        answer(ready_x.at[1], right)

    @pl.when(x_left < x)
    def _():
        answer(ready_x.at[0], left)

    @pl.when(core == 1)
    def _():
        answer(ready_core, other)

    for copy in later_loads:
        copy.start()

    @pl.when(core == 0)
    def _():
        pl.semaphore_wait(ready_core, 1)

    for copy in w_sends:
        copy.start()
    for copy in w_loads:
        copy.start()
    for copy in later_loads:
        copy.wait()

    def within(h):
        hc = columns(h)
        for b in range(2):
            rows = slice(b * BLOCK, (b + 1) * BLOCK)
            query = q[rows, hc]
            scores = lax.dot_general(
                query, k[rows, hc], (((1,), (1,)), ((), ())), preferred_element_type=F32
            )
            col = cb[rows, hc]
            between = jnp.concatenate([col, col], axis=1) - cumr[pl.ds(h, 1), rows]
            weights = jnp.exp(jnp.where(at_row >= at_col, jnp.minimum(between, 0.0), -1e30))
            attended = jnp.dot(
                (scores * weights).astype(BF16), v[rows, hc], preferred_element_type=F32
            )
            scaled = query.astype(F32) * jnp.exp(col)
            if b == 1:
                attended += jnp.dot(
                    scaled.astype(BF16), s_first[h], preferred_element_type=F32
                )
                scaled = query.astype(F32) * jnp.exp(col + cb[BLOCK - 1 : BLOCK, hc])
            qs[rows, hc] = scaled.astype(BF16)
            att[rows, hc] = attended
            gg[rows, hc] = gain[pl.ds(h, 1), :] * jax.nn.sigmoid(gate[rows, hc].astype(F32))

    @pl.loop(0, EARLY)
    def _(h):
        within(h)

    def row_copy(part, there):
        return remote(
            t_out.at[part],
            t_in.at[part, y],
            t_s.at[part, there],
            t_r.at[part, y],
            {"seq": there * NZ + z},
        )

    def decay_copy(there):
        return remote(
            rd_out, rd_in.at[y], rd_s.at[there], rd_r.at[y], {"seq": there * NZ + z}
        )

    def prefix_copy(part, there):
        return remote(
            p_out.at[part, there],
            p_in.at[part, z],
            s3.at[part, there],
            r3.at[part, z],
            {"seq": row0 + there},
        )

    def prefix(part, there):
        entering = jnp.exp(cl_pre[there : there + 1, :]) * rows_before[part] + w_pre[part, there]
        p_out[part, there] = entering.astype(BF16)

        @pl.when(there != z)
        def _():
            prefix_copy(part, there).start()

    for part in range(PARTS):
        state = jnp.zeros((PD, HD), F32)
        log = jnp.zeros((1, HD), F32)
        for there in range(NZ):
            w_pre[part, there] = state
            if part == 0:
                cl_pre[there : there + 1, :] = log

            @pl.when(there != z)
            def _():
                if part == 0:
                    remote(lt, ltb.at[there], lt_s.at[0], lt_r.at[there], other).wait_recv()
                remote(
                    s_end.at[part, 0], s_in.at[part, there], s1.at[0, 0], r1.at[part, there], other
                ).wait_recv()

            step = ltb[there, pl.ds(z, 1), :]
            state = jnp.exp(step) * state + s_in[part, there].astype(F32)
            log = log + step
        t_out[part] = state.astype(BF16)
        if part == 0:
            rd_out[...] = jnp.broadcast_to(log, (8, HD))
        for there in range(1, NY):

            @pl.when(there > y)
            def _():
                if part == 0:
                    pl.semaphore_wait(ready_y.at[there], 1)
                    decay_copy(there).start()
                row_copy(part, there).start()

    for part in range(PARTS):
        rows_before[part] = jnp.zeros((PD, HD), F32)
        for there in range(NY - 1):

            @pl.when(there < y)
            def _():
                if part == 0:
                    remote(rd_out, rd_in.at[there], rd_s.at[0], rd_r.at[there], other).wait_recv()
                remote(
                    t_out.at[0], t_in.at[part, there], t_s.at[0, 0], t_r.at[part, there], other
                ).wait_recv()
                rows_before[part] = jnp.exp(rd_in[there][0:1, :]) * rows_before[part] + t_in[
                    part, there
                ].astype(F32)

        for there in range(NZ // 2):
            prefix(part, there)
    for there in range(NZ // 2, NZ):
        for part in range(PARTS):
            prefix(part, there)
    for part in range(PARTS):
        p_in[part, z] = p_out[part, z]

    @pl.loop(EARLY, HEADS)
    def _(h):
        within(h)

    for copy in w_loads:
        copy.wait()
    for copy in w_sends:
        copy.wait_recv()
    for off in range(1, NZ):
        there = along_z(off)
        for part in range(PARTS):
            remote(
                p_out.at[0, 0], p_in.at[part, there], s3.at[0, 0], r3.at[part, there], other
            ).wait_recv()

    def tile(t):
        return pl.ds(pl.multiple_of(t * TILE, TILE), TILE)

    def hidden_copy(t):
        return remote(h_own.at[tile(t)], h_peer.at[tile(t)], h_s.at[t], h_r.at[t], other)

    def make_hidden(t):
        rows = tile(t)
        for h in range(HEADS):
            hc = slice(h * HD, (h + 1) * HD)
            entering = jnp.concatenate([p_in[part, h] for part in range(PARTS)], axis=0)
            attended = att[rows, hc] + jnp.dot(
                qs[rows, hc], entering, preferred_element_type=F32
            )
            square = jnp.mean(attended * attended, axis=1, keepdims=True)
            h_own[rows, hc] = (attended * lax.rsqrt(square + 1e-06) * gg[rows, hc]).astype(BF16)
        hidden_copy(t).start()

    def chunk(t, i):
        return jnp.dot(h_own[tile(t), :], w_own[i], preferred_element_type=F32) + jnp.dot(
            h_peer[tile(t), :], w_peer[i], preferred_element_type=F32
        )

    targets = (right, left)
    halves = (slice(0, HALF), slice(HALF, TILE))

    def first_copy(t, way):
        return remote(
            opp.at[t, way], fwd.at[way, t], m1_s.at[way, t], m1_r.at[way, t], targets[way]
        )

    def side_copy(t, way):
        return remote(
            side.at[way, t], fin.at[way, t, 1 - way], m2_s.at[way, t], m2_r.at[way, t], targets[way]
        )

    def passing_copy(t, way):
        return remote(
            passing.at[way, t], fin.at[way, t, way], m3_s.at[way, t], m3_r.at[way, t], targets[way]
        )

    def send_far(t):
        hidden_copy(t).wait_recv()
        far = chunk(t, x_opp).astype(BF16)
        for way in range(2):
            opp[t, way] = far[halves[way]]
            first_copy(t, way).start()

    def send_near(t):
        for way, i in enumerate((x_right, x_left)):
            near = chunk(t, i)
            side[way, t] = near[halves[1 - way]].astype(BF16)
            side_copy(t, way).start()
            held[way, t] = near[halves[way]]

    def pass_on(t):
        for way in range(2):
            first_copy(t, way).wait_recv()
            passing[way, t] = (held[way, t] + fwd[way, t].astype(F32)).astype(BF16)
            passing_copy(t, way).start()

    @pl.when(x_right > x)
    def _():
        pl.semaphore_wait(ready_x.at[0], 1)

    @pl.when(x_left > x)
    def _():
        pl.semaphore_wait(ready_x.at[1], 1)

    make_hidden(0)

    @pl.loop(0, NT)
    def _(t):
        @pl.when(t < NT - 1)
        def _():
            make_hidden(t + 1)

        send_far(t)

    @pl.loop(0, NT)
    def _(t):
        send_near(t)

        @pl.when(t > 0)
        def _():
            pass_on(t - 1)

    pass_on(NT - 1)

    @pl.loop(0, NT)
    def _(t):
        mine[t] = chunk(t, x)

    for off in range(1, NZ):
        lt_copy(off).wait_send()
        there = along_z(off)
        for part in range(PARTS):
            state_copy(part, there).wait_send()
            prefix_copy(part, there).wait_send()
    for there in range(1, NY):

        @pl.when(there > y)
        def _():
            decay_copy(there).wait_send()
            for part in range(PARTS):
                row_copy(part, there).wait_send()

    for copy in w_sends:
        copy.wait_send()

    @pl.loop(0, NT)
    def _(t):
        hidden_copy(t).wait_send()
        for way in range(2):
            first_copy(t, way).wait_send()
            side_copy(t, way).wait_send()
            passing_copy(t, way).wait_send()

    @pl.loop(0, NT)
    def _(t):
        for way in range(2):
            side_copy(t, way).wait_recv()
            passing_copy(t, way).wait_recv()
        for half in range(2):
            rows = pl.ds(pl.multiple_of(t * TILE + half * HALF, HALF), HALF)
            out[rows, :] = (
                mine[t, halves[half]]
                + fin[0, t, half].astype(F32)
                + fin[1, t, half].astype(F32)
            ).astype(BF16)


def per_device(queries, keys, values, log_decay, gate, norm_gain, w_out):
    vmem, dma = pltpu.VMEM, pltpu.SemaphoreType.DMA
    scratch = [
        vmem((ROWS, FEAT), BF16),
        vmem((ROWS, FEAT), BF16),
        vmem((ROWS, FEAT), BF16),
        vmem((HEADS, ROWS), F32),
        vmem((ROWS, FEAT), BF16),
        vmem((HEADS, HD), F32),
        vmem((NX, FEAT, CW), BF16),
        vmem((NX, FEAT, CW), BF16),
        vmem((ROWS, FEAT), F32),
        vmem((HEADS, ROWS), F32),
        vmem((ROWS, FEAT), F32),
        vmem((ROWS, FEAT), BF16),
        vmem((ROWS, FEAT), F32),
        vmem((ROWS, FEAT), BF16),
        vmem((ROWS, FEAT), BF16),
        vmem((HEADS, HD), F32),
        vmem((NZ, HEADS, HD), F32),
        vmem((PARTS, HEADS, PD, HD), BF16),
        vmem((HEADS, HD, HD), BF16),
        vmem((PARTS, NZ, PD, HD), BF16),
        vmem((PARTS, NZ, PD, HD), F32),
        vmem((NZ, HD), F32),
        vmem((PARTS, PD, HD), BF16),
        vmem((PARTS, NY, PD, HD), BF16),
        vmem((8, HD), F32),
        vmem((NY, 8, HD), F32),
        vmem((PARTS, PD, HD), F32),
        vmem((PARTS, NZ, PD, HD), BF16),
        vmem((PARTS, HEADS, PD, HD), BF16),
        vmem((NT, 2, HALF, CW), BF16),
        vmem((2, NT, HALF, CW), BF16),
        vmem((2, NT, HALF, CW), F32),
        vmem((2, NT, HALF, CW), BF16),
        vmem((NT, TILE, CW), F32),
        vmem((2, NT, HALF, CW), BF16),
        vmem((2, NT, 2, HALF, CW), BF16),
        dma((6 + NX,)),
        dma((NZ,)), dma((NZ,)),
        dma((PARTS, NZ)), dma((PARTS, NZ)),
        dma((PARTS, NY)), dma((PARTS, NY)),
        dma((NY,)), dma((NY,)),
        dma((PARTS, NZ)), dma((PARTS, NZ)),
        dma((NX,)), dma((NX,)),
        dma((NT,)), dma((NT,)),
        dma((2, NT)), dma((2, NT)),
        dma((2, NT)), dma((2, NT)),
        dma((2, NT)), dma((2, NT)),
        pltpu.SemaphoreType.REGULAR((NY,)),
        pltpu.SemaphoreType.REGULAR((2,)),
        pltpu.SemaphoreType.REGULAR,
    ]
    return pl.pallas_call(
        kernel,
        out_shape=pltpu.VMEM((ROWS, CW), BF16),
        in_specs=[pl.BlockSpec(memory_space=pl.ANY)] * 7,
        out_specs=pl.BlockSpec(memory_space=pltpu.VMEM),
        scratch_shapes=scratch,
        compiler_params=pltpu.CompilerParams(
            collective_id=0, has_side_effects=True, vmem_limit_bytes=56 * 1024 * 1024
        ),
        cost_estimate=pl.CostEstimate(
            flops=2 * ROWS * FEAT * (3072 + 2 * BLOCK + 2 * HD),
            bytes_accessed=11_000_000,
            transcendentals=ROWS * FEAT * 4,
        ),
    )(queries, keys, values, log_decay.T, gate, norm_gain.reshape(HEADS, HD), w_out)


def solution(mesh):
    placed = (
        P("seq", "head"),
        P("seq", "head"),
        P("seq", "head"),
        P("seq", "head"),
        P("seq", "head"),
        P("head"),
        P("head", None),
    )
    return jax.shard_map(
        per_device, mesh=mesh, in_specs=placed, out_specs=P("seq", "head"), check_vma=False
    )
```

```python
import jax
import jax.numpy as jnp
from jax import lax
from jax.experimental import pallas as pl
from jax.experimental.pallas import tpu as pltpu
from jax.sharding import PartitionSpec as P

HD = 128
BLOCK = 256
NX, NY, NZ = 4, 4, 8
ROWS = 512
HEADS = 8
FEAT = HEADS * HD
CW = 384
TILE = 128
NT = ROWS // TILE
PARTS = 2
PD = HD // PARTS
FAR_FIRST = (4, 5, 3, 6, 2, 7, 1)
HALF = TILE // 2
EARLY = 6

F32, BF16 = jnp.float32, jnp.bfloat16
EXACT = lax.Precision.HIGHEST
MESH = pl.DeviceIdType.MESH


def remote(src, dst, send_sem, recv_sem, device_id):
    return pltpu.make_async_remote_copy(
        src_ref=src,
        dst_ref=dst,
        send_sem=send_sem,
        recv_sem=recv_sem,
        device_id=device_id,
        device_id_type=MESH,
    )


def columns(index, width=HD):
    return pl.ds(pl.multiple_of(index * width, HD), width)


def kernel(
    q_hbm, k_hbm, v_hbm, ld_hbm, gate_hbm, gain_hbm, w_hbm,
    out,
    q, k, v, ld, gate, gain, w_own, w_peer,
    cb, cumr, att, qs, gg, h_own, h_peer,
    s_end, s_first, s_in, w_pre, cl_pre, t_out, t_in, rows_before, p_out, p_in,
    opp, side, held, fwd, mine, passing, fin,
    load_sem, s1, r1, t_s, t_r, s3, r3, w_s, w_r, h_s, h_r,
    m1_s, m1_r, m2_s, m2_r, m3_s, m3_r, ready_y, ready_x, ready_core,
):
    head, seq = lax.axis_index("head"), lax.axis_index("seq")
    z, y = lax.rem(seq, NZ), lax.div(seq, NZ)
    row0 = seq - z
    core, x = lax.rem(head, 2), lax.div(head, 2)
    other = {"head": head + 1 - 2 * core}
    x_right, x_left, x_opp = lax.rem(x + 1, NX), lax.rem(x + 3, NX), lax.rem(x + 2, NX)
    right, left = {"head": x_right * 2 + core}, {"head": x_left * 2 + core}

    def along_z(off):
        return lax.rem(z + off, NZ)

    def along_y(off):
        return lax.rem(y + off, NY)

    def load(i, src, dst):
        return pltpu.make_async_copy(src, dst, load_sem.at[i])

    ld_load = load(0, ld_hbm, ld)
    kv_loads = [load(1, k_hbm, k), load(2, v_hbm, v)]
    later_loads = [
        load(3, q_hbm, q),
        load(4, gate_hbm, gate),
        load(5, gain_hbm, gain),
    ]
    w_loads = [
        pltpu.make_async_copy(
            w_hbm.at[:, pl.ds(pl.multiple_of((2 * i + core) * CW, HD), CW)],
            w_own.at[i],
            load_sem.at[6 + i],
        )
        for i in range(NX)
    ]
    w_sends = [
        remote(
            w_hbm.at[:, pl.ds(pl.multiple_of((2 * i + 1 - core) * CW, HD), CW)],
            w_peer.at[i],
            w_s.at[i],
            w_r.at[i],
            other,
        )
        for i in range(NX)
    ]

    barrier = pltpu.get_barrier_semaphore()

    def greet(device):
        pl.semaphore_signal(barrier, inc=1, device_id=device, device_id_type=MESH)

    def answer(sem, device):
        pl.semaphore_signal(sem, inc=1, device_id=device, device_id_type=MESH)

    for off in FAR_FIRST:
        greet({"seq": row0 + along_z(off)})
    ld_load.start()
    for copy in kv_loads:
        copy.start()
    for there in range(1, NY):

        @pl.when(there > y)
        def _():
            greet({"seq": there * NZ + z})

    @pl.when(x_right > x)
    def _():
        greet(right)

    @pl.when(x_left > x)
    def _():
        greet(left)

    @pl.when(core == 0)
    def _():
        greet(other)

    greeted = NZ - 1 + y + core + jnp.where(x_right < x, 1, 0) + jnp.where(x_left < x, 1, 0)

    at_row = lax.broadcasted_iota(jnp.int32, (BLOCK, BLOCK), 0)
    at_col = lax.broadcasted_iota(jnp.int32, (BLOCK, BLOCK), 1)
    lower = jnp.where(at_row >= at_col, 1.0, 0.0).astype(F32)
    upper = jnp.where(at_row <= at_col, 1.0, 0.0).astype(F32)
    ld_load.wait()
    for b in range(2):
        rows = slice(b * BLOCK, (b + 1) * BLOCK)
        decay = ld[:, rows]
        cum = lax.dot_general(
            lower, decay, (((1,), (1,)), ((), ())), precision=EXACT, preferred_element_type=F32
        )
        cumr[:, rows] = jnp.dot(decay, upper, precision=EXACT, preferred_element_type=F32)
        for h in range(HEADS):
            cb[rows, h * HD : (h + 1) * HD] = jnp.broadcast_to(cum[:, h : h + 1], (BLOCK, HD))

    def rows_of(part):
        return PD + 16 if part == 0 else PD

    row_at = lax.broadcasted_iota(jnp.int32, (16, HD), 0)

    def split_rows(log):
        high = log.astype(BF16).astype(F32)
        middle = (log - high).astype(BF16).astype(F32)
        low = log - high - middle
        return jnp.where(
            row_at == 0,
            high,
            jnp.where(row_at == 1, middle, jnp.where(row_at == 2, low, 0.0)),
        ).astype(BF16)

    def joined_rows(split):
        wide = split.astype(F32)
        return wide[0:1] + wide[1:2] + wide[2:3]

    def state_copy(part, h):
        return remote(
            s_end.at[part, h, 0 : rows_of(part)],
            s_in.at[part, z, 0 : rows_of(part)],
            s1.at[part, h],
            r1.at[part, z],
            {"seq": row0 + h},
        )

    for copy in kv_loads:
        copy.wait()
    for h in range(HEADS):
        hc = slice(h * HD, (h + 1) * HD)
        ends = []
        for b in range(2):
            rows = slice(b * BLOCK, (b + 1) * BLOCK)
            total = cb[(b + 1) * BLOCK - 1 : (b + 1) * BLOCK, hc]
            weighted = (k[rows, hc].astype(F32) * jnp.exp(total - cb[rows, hc])).astype(BF16)
            ends.append(
                lax.dot_general(
                    weighted, v[rows, hc], (((0,), (0,)), ((), ())), preferred_element_type=F32
                )
            )
        s_first[h] = ends[0].astype(BF16)
        whole = (jnp.exp(cb[ROWS - 1 : ROWS, hc]) * ends[0] + ends[1]).astype(BF16)
        for part in range(PARTS):
            s_end[part, h, 0:PD] = whole[part * PD : (part + 1) * PD]
        s_end[0, h, PD : PD + 16] = split_rows(cb[BLOCK - 1 : BLOCK, hc] + cb[ROWS - 1 : ROWS, hc])

    pl.semaphore_wait(barrier, greeted)
    for part in range(PARTS):
        for off in FAR_FIRST:
            state_copy(part, along_z(off)).start()
    for part in range(PARTS):
        s_in[part, z] = s_end[part, z]
    for there in range(NY - 1):

        @pl.when(there < y)
        def _():
            answer(ready_y.at[y], {"seq": there * NZ + z})

    @pl.when(x_right < x)
    def _():
        answer(ready_x.at[1], right)

    @pl.when(x_left < x)
    def _():
        answer(ready_x.at[0], left)

    @pl.when(core == 1)
    def _():
        answer(ready_core, other)

    for copy in later_loads:
        copy.start()

    @pl.when(core == 0)
    def _():
        pl.semaphore_wait(ready_core, 1)

    for copy in w_sends:
        copy.start()
    for copy in w_loads:
        copy.start()
    for copy in later_loads:
        copy.wait()

    def within(h):
        hc = columns(h)
        for b in range(2):
            rows = slice(b * BLOCK, (b + 1) * BLOCK)
            query = q[rows, hc]
            scores = lax.dot_general(
                query, k[rows, hc], (((1,), (1,)), ((), ())), preferred_element_type=F32
            )
            col = cb[rows, hc]
            between = jnp.concatenate([col, col], axis=1) - cumr[pl.ds(h, 1), rows]
            weights = jnp.exp(jnp.where(at_row >= at_col, jnp.minimum(between, 0.0), -1e30))
            attended = jnp.dot(
                (scores * weights).astype(BF16), v[rows, hc], preferred_element_type=F32
            )
            scaled = query.astype(F32) * jnp.exp(col)
            if b == 1:
                attended += jnp.dot(
                    scaled.astype(BF16), s_first[h], preferred_element_type=F32
                )
                scaled = query.astype(F32) * jnp.exp(col + cb[BLOCK - 1 : BLOCK, hc])
            qs[rows, hc] = scaled.astype(BF16)
            att[rows, hc] = attended
            gg[rows, hc] = gain[pl.ds(h, 1), :] * jax.nn.sigmoid(gate[rows, hc].astype(F32))

    @pl.loop(0, EARLY)
    def _(h):
        within(h)

    def row_copy(part, there):
        return remote(
            t_out.at[part, 0 : rows_of(part)],
            t_in.at[part, y, 0 : rows_of(part)],
            t_s.at[part, there],
            t_r.at[part, y],
            {"seq": there * NZ + z},
        )

    def prefix_copy(part, there):
        return remote(
            p_out.at[part, there],
            p_in.at[part, z],
            s3.at[part, there],
            r3.at[part, z],
            {"seq": row0 + there},
        )

    def prefix(part, there):
        entering = jnp.exp(cl_pre[there : there + 1, :]) * rows_before[part] + w_pre[part, there]
        p_out[part, there] = entering.astype(BF16)

        @pl.when(there != z)
        def _():
            prefix_copy(part, there).start()

    for part in range(PARTS):
        state = jnp.zeros((PD, HD), F32)
        log = jnp.zeros((1, HD), F32)
        for there in range(NZ):
            w_pre[part, there] = state
            if part == 0:
                cl_pre[there : there + 1, :] = log

            @pl.when(there != z)
            def _():
                remote(
                    s_end.at[part, 0, 0 : rows_of(part)],
                    s_in.at[part, there, 0 : rows_of(part)],
                    s1.at[0, 0],
                    r1.at[part, there],
                    other,
                ).wait_recv()

            step = joined_rows(s_in[0, there, PD : PD + 16])
            state = jnp.exp(step) * state + s_in[part, there, 0:PD].astype(F32)
            log = log + step
        t_out[part, 0:PD] = state.astype(BF16)
        if part == 0:
            t_out[0, PD : PD + 16] = split_rows(log)
        for there in range(1, NY):

            @pl.when(there > y)
            def _():
                if part == 0:
                    pl.semaphore_wait(ready_y.at[there], 1)
                row_copy(part, there).start()

    for part in range(PARTS):
        rows_before[part] = jnp.zeros((PD, HD), F32)
        for there in range(NY - 1):

            @pl.when(there < y)
            def _():
                remote(
                    t_out.at[part, 0 : rows_of(part)],
                    t_in.at[part, there, 0 : rows_of(part)],
                    t_s.at[0, 0],
                    t_r.at[part, there],
                    other,
                ).wait_recv()
                rows_before[part] = jnp.exp(
                    joined_rows(t_in[0, there, PD : PD + 16])
                ) * rows_before[part] + t_in[part, there, 0:PD].astype(F32)

        for there in range(NZ // 2):
            prefix(part, there)
    for there in range(NZ // 2, NZ):
        for part in range(PARTS):
            prefix(part, there)
    for part in range(PARTS):
        p_in[part, z] = p_out[part, z]

    @pl.loop(EARLY, HEADS)
    def _(h):
        within(h)

    for copy in w_loads:
        copy.wait()
    for copy in w_sends:
        copy.wait_recv()
    for off in range(1, NZ):
        there = along_z(off)
        for part in range(PARTS):
            remote(
                p_out.at[0, 0], p_in.at[part, there], s3.at[0, 0], r3.at[part, there], other
            ).wait_recv()

    def tile(t):
        return pl.ds(pl.multiple_of(t * TILE, TILE), TILE)

    def hidden_copy(t):
        return remote(h_own.at[tile(t)], h_peer.at[tile(t)], h_s.at[t], h_r.at[t], other)

    def make_hidden(t):
        rows = tile(t)
        for h in range(HEADS):
            hc = slice(h * HD, (h + 1) * HD)
            entering = jnp.concatenate([p_in[part, h] for part in range(PARTS)], axis=0)
            attended = att[rows, hc] + jnp.dot(
                qs[rows, hc], entering, preferred_element_type=F32
            )
            square = jnp.mean(attended * attended, axis=1, keepdims=True)
            h_own[rows, hc] = (attended * lax.rsqrt(square + 1e-06) * gg[rows, hc]).astype(BF16)
        hidden_copy(t).start()

    def chunk(t, i):
        return jnp.dot(h_own[tile(t), :], w_own[i], preferred_element_type=F32) + jnp.dot(
            h_peer[tile(t), :], w_peer[i], preferred_element_type=F32
        )

    targets = (right, left)
    halves = (slice(0, HALF), slice(HALF, TILE))

    def first_copy(t, way):
        return remote(
            opp.at[t, way], fwd.at[way, t], m1_s.at[way, t], m1_r.at[way, t], targets[way]
        )

    def side_copy(t, way):
        return remote(
            side.at[way, t], fin.at[way, t, 1 - way], m2_s.at[way, t], m2_r.at[way, t], targets[way]
        )

    def passing_copy(t, way):
        return remote(
            passing.at[way, t], fin.at[way, t, way], m3_s.at[way, t], m3_r.at[way, t], targets[way]
        )

    def send_far(t):
        hidden_copy(t).wait_recv()
        far = chunk(t, x_opp).astype(BF16)
        for way in range(2):
            opp[t, way] = far[halves[way]]
            first_copy(t, way).start()

    def send_near(t):
        for way, i in enumerate((x_right, x_left)):
            near = chunk(t, i)
            side[way, t] = near[halves[1 - way]].astype(BF16)
            side_copy(t, way).start()
            held[way, t] = near[halves[way]]

    def pass_on(t):
        for way in range(2):
            first_copy(t, way).wait_recv()
            passing[way, t] = (held[way, t] + fwd[way, t].astype(F32)).astype(BF16)
            passing_copy(t, way).start()

    @pl.when(x_right > x)
    def _():
        pl.semaphore_wait(ready_x.at[0], 1)

    @pl.when(x_left > x)
    def _():
        pl.semaphore_wait(ready_x.at[1], 1)

    make_hidden(0)

    @pl.loop(0, NT)
    def _(t):
        @pl.when(t < NT - 1)
        def _():
            make_hidden(t + 1)

        send_far(t)

    @pl.loop(0, NT)
    def _(t):
        send_near(t)

        @pl.when(t > 0)
        def _():
            pass_on(t - 1)

    pass_on(NT - 1)

    @pl.loop(0, NT)
    def _(t):
        mine[t] = chunk(t, x)

    for off in range(1, NZ):
        there = along_z(off)
        for part in range(PARTS):
            state_copy(part, there).wait_send()
            prefix_copy(part, there).wait_send()
    for there in range(1, NY):

        @pl.when(there > y)
        def _():
            for part in range(PARTS):
                row_copy(part, there).wait_send()

    for copy in w_sends:
        copy.wait_send()

    @pl.loop(0, NT)
    def _(t):
        hidden_copy(t).wait_send()
        for way in range(2):
            first_copy(t, way).wait_send()
            side_copy(t, way).wait_send()
            passing_copy(t, way).wait_send()

    @pl.loop(0, NT)
    def _(t):
        for way in range(2):
            side_copy(t, way).wait_recv()
            passing_copy(t, way).wait_recv()
        for half in range(2):
            rows = pl.ds(pl.multiple_of(t * TILE + half * HALF, HALF), HALF)
            out[rows, :] = (
                mine[t, halves[half]]
                + fin[0, t, half].astype(F32)
                + fin[1, t, half].astype(F32)
            ).astype(BF16)


def per_device(queries, keys, values, log_decay, gate, norm_gain, w_out):
    vmem, dma = pltpu.VMEM, pltpu.SemaphoreType.DMA
    scratch = [
        vmem((ROWS, FEAT), BF16),
        vmem((ROWS, FEAT), BF16),
        vmem((ROWS, FEAT), BF16),
        vmem((HEADS, ROWS), F32),
        vmem((ROWS, FEAT), BF16),
        vmem((HEADS, HD), F32),
        vmem((NX, FEAT, CW), BF16),
        vmem((NX, FEAT, CW), BF16),
        vmem((ROWS, FEAT), F32),
        vmem((HEADS, ROWS), F32),
        vmem((ROWS, FEAT), F32),
        vmem((ROWS, FEAT), BF16),
        vmem((ROWS, FEAT), F32),
        vmem((ROWS, FEAT), BF16),
        vmem((ROWS, FEAT), BF16),
        vmem((PARTS, HEADS, PD + 16, HD), BF16),
        vmem((HEADS, HD, HD), BF16),
        vmem((PARTS, NZ, PD + 16, HD), BF16),
        vmem((PARTS, NZ, PD, HD), F32),
        vmem((NZ, HD), F32),
        vmem((PARTS, PD + 16, HD), BF16),
        vmem((PARTS, NY, PD + 16, HD), BF16),
        vmem((PARTS, PD, HD), F32),
        vmem((PARTS, NZ, PD, HD), BF16),
        vmem((PARTS, HEADS, PD, HD), BF16),
        vmem((NT, 2, HALF, CW), BF16),
        vmem((2, NT, HALF, CW), BF16),
        vmem((2, NT, HALF, CW), F32),
        vmem((2, NT, HALF, CW), BF16),
        vmem((NT, TILE, CW), F32),
        vmem((2, NT, HALF, CW), BF16),
        vmem((2, NT, 2, HALF, CW), BF16),
        dma((6 + NX,)),
        dma((PARTS, NZ)), dma((PARTS, NZ)),
        dma((PARTS, NY)), dma((PARTS, NY)),
        dma((PARTS, NZ)), dma((PARTS, NZ)),
        dma((NX,)), dma((NX,)),
        dma((NT,)), dma((NT,)),
        dma((2, NT)), dma((2, NT)),
        dma((2, NT)), dma((2, NT)),
        dma((2, NT)), dma((2, NT)),
        pltpu.SemaphoreType.REGULAR((NY,)),
        pltpu.SemaphoreType.REGULAR((2,)),
        pltpu.SemaphoreType.REGULAR,
    ]
    return pl.pallas_call(
        kernel,
        out_shape=pltpu.VMEM((ROWS, CW), BF16),
        in_specs=[pl.BlockSpec(memory_space=pl.ANY)] * 7,
        out_specs=pl.BlockSpec(memory_space=pltpu.VMEM),
        scratch_shapes=scratch,
        compiler_params=pltpu.CompilerParams(
            collective_id=0, has_side_effects=True, vmem_limit_bytes=56 * 1024 * 1024
        ),
        cost_estimate=pl.CostEstimate(
            flops=2 * ROWS * FEAT * (3072 + 2 * BLOCK + 2 * HD),
            bytes_accessed=11_000_000,
            transcendentals=ROWS * FEAT * 4,
        ),
    )(queries, keys, values, log_decay.T, gate, norm_gain.reshape(HEADS, HD), w_out)


def solution(mesh):
    placed = (
        P("seq", "head"),
        P("seq", "head"),
        P("seq", "head"),
        P("seq", "head"),
        P("seq", "head"),
        P("head"),
        P("head", None),
    )
    return jax.shard_map(
        per_device, mesh=mesh, in_specs=placed, out_specs=P("seq", "head"), check_vma=False
    )
```

```python
import jax
import jax.numpy as jnp
from jax import lax
from jax.experimental import pallas as pl
from jax.experimental.pallas import tpu as pltpu
from jax.sharding import PartitionSpec as P

HD = 128
BLOCK = 256
NX, NY, NZ = 4, 4, 8
ROWS = 512
HEADS = 8
FEAT = HEADS * HD
CW = 384
TILE = 128
NT = ROWS // TILE
PARTS = 2
PD = HD // PARTS
FAR_FIRST = (4, 5, 3, 6, 2, 7, 1)
HALF = TILE // 2
EARLY = 8

F32, BF16 = jnp.float32, jnp.bfloat16
EXACT = lax.Precision.HIGHEST
MESH = pl.DeviceIdType.MESH


def remote(src, dst, send_sem, recv_sem, device_id):
    return pltpu.make_async_remote_copy(
        src_ref=src,
        dst_ref=dst,
        send_sem=send_sem,
        recv_sem=recv_sem,
        device_id=device_id,
        device_id_type=MESH,
    )


def columns(index, width=HD):
    return pl.ds(pl.multiple_of(index * width, HD), width)


def kernel(
    q_hbm, k_hbm, v_hbm, ld_hbm, gate_hbm, gain_hbm, w_hbm,
    out,
    q, k, v, ld, gate, gain, w_own, w_peer,
    cb, cumr, att, qs, gg, h_own, h_peer,
    s_end, s_first, s_in, w_pre, cl_pre, t_out, t_in, rows_before, p_out, p_in,
    opp, side, held, fwd, mine, passing, fin,
    load_sem, s1, r1, t_s, t_r, s3, r3, w_s, w_r, h_s, h_r,
    m1_s, m1_r, m2_s, m2_r, m3_s, m3_r, ready_y, ready_x, ready_core,
):
    head, seq = lax.axis_index("head"), lax.axis_index("seq")
    z, y = lax.rem(seq, NZ), lax.div(seq, NZ)
    row0 = seq - z
    core, x = lax.rem(head, 2), lax.div(head, 2)
    other = {"head": head + 1 - 2 * core}
    x_right, x_left, x_opp = lax.rem(x + 1, NX), lax.rem(x + 3, NX), lax.rem(x + 2, NX)
    right, left = {"head": x_right * 2 + core}, {"head": x_left * 2 + core}

    def along_z(off):
        return lax.rem(z + off, NZ)

    def along_y(off):
        return lax.rem(y + off, NY)

    def load(i, src, dst):
        return pltpu.make_async_copy(src, dst, load_sem.at[i])

    ld_load = load(0, ld_hbm, ld)
    kv_loads = [load(1, k_hbm, k), load(2, v_hbm, v)]
    later_loads = [
        load(3, q_hbm, q),
        load(4, gate_hbm, gate),
        load(5, gain_hbm, gain),
    ]
    w_loads = [
        pltpu.make_async_copy(
            w_hbm.at[:, pl.ds(pl.multiple_of((2 * i + core) * CW, HD), CW)],
            w_own.at[i],
            load_sem.at[6 + i],
        )
        for i in range(NX)
    ]
    w_sends = [
        remote(
            w_hbm.at[:, pl.ds(pl.multiple_of((2 * i + 1 - core) * CW, HD), CW)],
            w_peer.at[i],
            w_s.at[i],
            w_r.at[i],
            other,
        )
        for i in range(NX)
    ]

    barrier = pltpu.get_barrier_semaphore()

    def greet(device):
        pl.semaphore_signal(barrier, inc=1, device_id=device, device_id_type=MESH)

    def answer(sem, device):
        pl.semaphore_signal(sem, inc=1, device_id=device, device_id_type=MESH)

    for off in FAR_FIRST:
        greet({"seq": row0 + along_z(off)})
    ld_load.start()
    for copy in kv_loads:
        copy.start()
    for there in range(1, NY):

        @pl.when(there > y)
        def _():
            greet({"seq": there * NZ + z})

    @pl.when(x_right > x)
    def _():
        greet(right)

    @pl.when(x_left > x)
    def _():
        greet(left)

    @pl.when(core == 0)
    def _():
        greet(other)

    greeted = NZ - 1 + y + core + jnp.where(x_right < x, 1, 0) + jnp.where(x_left < x, 1, 0)

    at_row = lax.broadcasted_iota(jnp.int32, (BLOCK, BLOCK), 0)
    at_col = lax.broadcasted_iota(jnp.int32, (BLOCK, BLOCK), 1)
    lower = jnp.where(at_row >= at_col, 1.0, 0.0).astype(F32)
    upper = jnp.where(at_row <= at_col, 1.0, 0.0).astype(F32)
    ld_load.wait()
    for b in range(2):
        rows = slice(b * BLOCK, (b + 1) * BLOCK)
        decay = ld[:, rows]
        cum = lax.dot_general(
            lower, decay, (((1,), (1,)), ((), ())), precision=EXACT, preferred_element_type=F32
        )
        cumr[:, rows] = jnp.dot(decay, upper, precision=EXACT, preferred_element_type=F32)
        for h in range(HEADS):
            cb[rows, h * HD : (h + 1) * HD] = jnp.broadcast_to(cum[:, h : h + 1], (BLOCK, HD))

    def rows_of(part):
        return PD + 16 if part == 0 else PD

    row_at = lax.broadcasted_iota(jnp.int32, (16, HD), 0)

    def split_rows(log):
        high = log.astype(BF16).astype(F32)
        middle = (log - high).astype(BF16).astype(F32)
        low = log - high - middle
        return jnp.where(
            row_at == 0,
            high,
            jnp.where(row_at == 1, middle, jnp.where(row_at == 2, low, 0.0)),
        ).astype(BF16)

    def joined_rows(split):
        wide = split.astype(F32)
        return wide[0:1] + wide[1:2] + wide[2:3]

    def state_copy(part, h):
        return remote(
            s_end.at[part, h, 0 : rows_of(part)],
            s_in.at[part, z, 0 : rows_of(part)],
            s1.at[part, h],
            r1.at[part, z],
            {"seq": row0 + h},
        )

    for copy in kv_loads:
        copy.wait()
    for h in range(HEADS):
        hc = slice(h * HD, (h + 1) * HD)
        ends = []
        for b in range(2):
            rows = slice(b * BLOCK, (b + 1) * BLOCK)
            total = cb[(b + 1) * BLOCK - 1 : (b + 1) * BLOCK, hc]
            weighted = (k[rows, hc].astype(F32) * jnp.exp(total - cb[rows, hc])).astype(BF16)
            ends.append(
                lax.dot_general(
                    weighted, v[rows, hc], (((0,), (0,)), ((), ())), preferred_element_type=F32
                )
            )
        s_first[h] = ends[0].astype(BF16)
        whole = (jnp.exp(cb[ROWS - 1 : ROWS, hc]) * ends[0] + ends[1]).astype(BF16)
        for part in range(PARTS):
            s_end[part, h, 0:PD] = whole[part * PD : (part + 1) * PD]
        s_end[0, h, PD : PD + 16] = split_rows(cb[BLOCK - 1 : BLOCK, hc] + cb[ROWS - 1 : ROWS, hc])

    pl.semaphore_wait(barrier, greeted)
    for part in range(PARTS):
        for off in FAR_FIRST:
            state_copy(part, along_z(off)).start()
    for part in range(PARTS):
        s_in[part, z] = s_end[part, z]
    for there in range(NY - 1):

        @pl.when(there < y)
        def _():
            answer(ready_y.at[y], {"seq": there * NZ + z})

    @pl.when(x_right < x)
    def _():
        answer(ready_x.at[1], right)

    @pl.when(x_left < x)
    def _():
        answer(ready_x.at[0], left)

    @pl.when(core == 1)
    def _():
        answer(ready_core, other)

    for copy in later_loads:
        copy.start()

    @pl.when(core == 0)
    def _():
        pl.semaphore_wait(ready_core, 1)

    for copy in w_sends:
        copy.start()
    for copy in w_loads:
        copy.start()
    for copy in later_loads:
        copy.wait()

    def within(h):
        hc = columns(h)
        for b in range(2):
            rows = slice(b * BLOCK, (b + 1) * BLOCK)
            query = q[rows, hc]
            scores = lax.dot_general(
                query, k[rows, hc], (((1,), (1,)), ((), ())), preferred_element_type=F32
            )
            col = cb[rows, hc]
            between = jnp.concatenate([col, col], axis=1) - cumr[pl.ds(h, 1), rows]
            weights = jnp.exp(jnp.where(at_row >= at_col, jnp.minimum(between, 0.0), -1e30))
            attended = jnp.dot(
                (scores * weights).astype(BF16), v[rows, hc], preferred_element_type=F32
            )
            scaled = query.astype(F32) * jnp.exp(col)
            if b == 1:
                attended += jnp.dot(
                    scaled.astype(BF16), s_first[h], preferred_element_type=F32
                )
                scaled = query.astype(F32) * jnp.exp(col + cb[BLOCK - 1 : BLOCK, hc])
            qs[rows, hc] = scaled.astype(BF16)
            att[rows, hc] = attended
            gg[rows, hc] = gain[pl.ds(h, 1), :] * jax.nn.sigmoid(gate[rows, hc].astype(F32))

    @pl.loop(0, EARLY)
    def _(h):
        within(h)

    def row_copy(part, there):
        return remote(
            t_out.at[part, 0 : rows_of(part)],
            t_in.at[part, y, 0 : rows_of(part)],
            t_s.at[part, there],
            t_r.at[part, y],
            {"seq": there * NZ + z},
        )

    def prefix_copy(part, there):
        return remote(
            p_out.at[part, there],
            p_in.at[part, z],
            s3.at[part, there],
            r3.at[part, z],
            {"seq": row0 + there},
        )

    def enter(part, there):
        entering = jnp.exp(cl_pre[there : there + 1, :]) * rows_before[part] + w_pre[part, there]
        p_out[part, there] = entering.astype(BF16)

    def send_prefix(part, there):
        @pl.when(there != z)
        def _():
            prefix_copy(part, there).start()

    for part in range(PARTS):
        state = jnp.zeros((PD, HD), F32)
        log = jnp.zeros((1, HD), F32)
        for first in range(0, NZ, NZ // 2):
            for there in range(first, first + NZ // 2):

                @pl.when(there != z)
                def _():
                    remote(
                        s_end.at[part, 0, 0 : rows_of(part)],
                        s_in.at[part, there, 0 : rows_of(part)],
                        s1.at[0, 0],
                        r1.at[part, there],
                        other,
                    ).wait_recv()

            for there in range(first, first + NZ // 2):
                w_pre[part, there] = state
                if part == 0:
                    cl_pre[there : there + 1, :] = log
                step = joined_rows(s_in[0, there, PD : PD + 16])
                state = jnp.exp(step) * state + s_in[part, there, 0:PD].astype(F32)
                log = log + step
        t_out[part, 0:PD] = state.astype(BF16)
        if part == 0:
            t_out[0, PD : PD + 16] = split_rows(log)
        for there in range(1, NY):

            @pl.when(there > y)
            def _():
                if part == 0:
                    pl.semaphore_wait(ready_y.at[there], 1)
                row_copy(part, there).start()

    for part in range(PARTS):
        rows_before[part] = jnp.zeros((PD, HD), F32)
        for there in range(NY - 1):

            @pl.when(there < y)
            def _():
                remote(
                    t_out.at[part, 0 : rows_of(part)],
                    t_in.at[part, there, 0 : rows_of(part)],
                    t_s.at[0, 0],
                    t_r.at[part, there],
                    other,
                ).wait_recv()
                rows_before[part] = jnp.exp(
                    joined_rows(t_in[0, there, PD : PD + 16])
                ) * rows_before[part] + t_in[part, there, 0:PD].astype(F32)

        for there in range(NZ // 2):
            enter(part, there)
        for there in range(NZ // 2):
            send_prefix(part, there)
    for part in range(PARTS):
        for there in range(NZ // 2, NZ):
            enter(part, there)
        for there in range(NZ // 2, NZ):
            send_prefix(part, there)
    for part in range(PARTS):
        p_in[part, z] = p_out[part, z]

    @pl.loop(EARLY, HEADS)
    def _(h):
        within(h)

    for copy in w_loads:
        copy.wait()
    for copy in w_sends:
        copy.wait_recv()
    for off in range(1, NZ):
        there = along_z(off)
        for part in range(PARTS):
            remote(
                p_out.at[0, 0], p_in.at[part, there], s3.at[0, 0], r3.at[part, there], other
            ).wait_recv()

    def tile(t):
        return pl.ds(pl.multiple_of(t * TILE, TILE), TILE)

    def hidden_copy(t):
        return remote(h_own.at[tile(t)], h_peer.at[tile(t)], h_s.at[t], h_r.at[t], other)

    def make_hidden(t):
        rows = tile(t)
        for h in range(HEADS):
            hc = slice(h * HD, (h + 1) * HD)
            entering = jnp.concatenate([p_in[part, h] for part in range(PARTS)], axis=0)
            attended = att[rows, hc] + jnp.dot(
                qs[rows, hc], entering, preferred_element_type=F32
            )
            square = jnp.mean(attended * attended, axis=1, keepdims=True)
            h_own[rows, hc] = (attended * lax.rsqrt(square + 1e-06) * gg[rows, hc]).astype(BF16)
        hidden_copy(t).start()

    def chunk(t, i):
        hidden = jnp.concatenate([h_own[tile(t), :], h_peer[tile(t), :]], axis=1)
        return jnp.dot(
            hidden,
            jnp.concatenate([w_own[i], w_peer[i]], axis=0),
            preferred_element_type=F32,
        )

    targets = (right, left)
    halves = (slice(0, HALF), slice(HALF, TILE))

    def first_copy(t, way):
        return remote(
            opp.at[t, way], fwd.at[way, t], m1_s.at[way, t], m1_r.at[way, t], targets[way]
        )

    def side_copy(t, way):
        return remote(
            side.at[way, t], fin.at[way, t, 1 - way], m2_s.at[way, t], m2_r.at[way, t], targets[way]
        )

    def passing_copy(t, way):
        return remote(
            passing.at[way, t], fin.at[way, t, way], m3_s.at[way, t], m3_r.at[way, t], targets[way]
        )

    def send_far(t):
        hidden_copy(t).wait_recv()
        far = chunk(t, x_opp).astype(BF16)
        for way in range(2):
            opp[t, way] = far[halves[way]]
            first_copy(t, way).start()

    def send_near(t):
        for way, i in ((1, x_left), (0, x_right)):
            near = chunk(t, i)
            side[way, t] = near[halves[1 - way]].astype(BF16)
            side_copy(t, way).start()
            held[way, t] = near[halves[way]]

    def pass_on(t):
        for way in range(2):
            first_copy(t, way).wait_recv()
            passing[way, t] = (held[way, t] + fwd[way, t].astype(F32)).astype(BF16)
            passing_copy(t, way).start()

    @pl.when(x_right > x)
    def _():
        pl.semaphore_wait(ready_x.at[0], 1)

    @pl.when(x_left > x)
    def _():
        pl.semaphore_wait(ready_x.at[1], 1)

    make_hidden(0)

    @pl.loop(0, NT)
    def _(t):
        @pl.when(t < NT - 1)
        def _():
            make_hidden(t + 1)

        send_far(t)

    @pl.loop(0, NT)
    def _(t):
        send_near(t)

        @pl.when(t > 0)
        def _():
            pass_on(t - 1)

    pass_on(NT - 1)

    @pl.loop(0, NT)
    def _(t):
        mine[t] = chunk(t, x)

    for off in range(1, NZ):
        there = along_z(off)
        for part in range(PARTS):
            state_copy(part, there).wait_send()
            prefix_copy(part, there).wait_send()
    for there in range(1, NY):

        @pl.when(there > y)
        def _():
            for part in range(PARTS):
                row_copy(part, there).wait_send()

    for copy in w_sends:
        copy.wait_send()

    @pl.loop(0, NT)
    def _(t):
        hidden_copy(t).wait_send()
        for way in range(2):
            first_copy(t, way).wait_send()
            side_copy(t, way).wait_send()
            passing_copy(t, way).wait_send()

    @pl.loop(0, NT)
    def _(t):
        for way in range(2):
            side_copy(t, way).wait_recv()
            passing_copy(t, way).wait_recv()
        for half in range(2):
            rows = pl.ds(pl.multiple_of(t * TILE + half * HALF, HALF), HALF)
            out[rows, :] = (
                mine[t, halves[half]]
                + fin[0, t, half].astype(F32)
                + fin[1, t, half].astype(F32)
            ).astype(BF16)


def per_device(queries, keys, values, log_decay, gate, norm_gain, w_out):
    vmem, dma = pltpu.VMEM, pltpu.SemaphoreType.DMA
    scratch = [
        vmem((ROWS, FEAT), BF16),
        vmem((ROWS, FEAT), BF16),
        vmem((ROWS, FEAT), BF16),
        vmem((HEADS, ROWS), F32),
        vmem((ROWS, FEAT), BF16),
        vmem((HEADS, HD), F32),
        vmem((NX, FEAT, CW), BF16),
        vmem((NX, FEAT, CW), BF16),
        vmem((ROWS, FEAT), F32),
        vmem((HEADS, ROWS), F32),
        vmem((ROWS, FEAT), F32),
        vmem((ROWS, FEAT), BF16),
        vmem((ROWS, FEAT), F32),
        vmem((ROWS, FEAT), BF16),
        vmem((ROWS, FEAT), BF16),
        vmem((PARTS, HEADS, PD + 16, HD), BF16),
        vmem((HEADS, HD, HD), BF16),
        vmem((PARTS, NZ, PD + 16, HD), BF16),
        vmem((PARTS, NZ, PD, HD), F32),
        vmem((NZ, HD), F32),
        vmem((PARTS, PD + 16, HD), BF16),
        vmem((PARTS, NY, PD + 16, HD), BF16),
        vmem((PARTS, PD, HD), F32),
        vmem((PARTS, NZ, PD, HD), BF16),
        vmem((PARTS, HEADS, PD, HD), BF16),
        vmem((NT, 2, HALF, CW), BF16),
        vmem((2, NT, HALF, CW), BF16),
        vmem((2, NT, HALF, CW), F32),
        vmem((2, NT, HALF, CW), BF16),
        vmem((NT, TILE, CW), F32),
        vmem((2, NT, HALF, CW), BF16),
        vmem((2, NT, 2, HALF, CW), BF16),
        dma((6 + NX,)),
        dma((PARTS, NZ)), dma((PARTS, NZ)),
        dma((PARTS, NY)), dma((PARTS, NY)),
        dma((PARTS, NZ)), dma((PARTS, NZ)),
        dma((NX,)), dma((NX,)),
        dma((NT,)), dma((NT,)),
        dma((2, NT)), dma((2, NT)),
        dma((2, NT)), dma((2, NT)),
        dma((2, NT)), dma((2, NT)),
        pltpu.SemaphoreType.REGULAR((NY,)),
        pltpu.SemaphoreType.REGULAR((2,)),
        pltpu.SemaphoreType.REGULAR,
    ]
    return pl.pallas_call(
        kernel,
        out_shape=pltpu.VMEM((ROWS, CW), BF16),
        in_specs=[pl.BlockSpec(memory_space=pl.ANY)] * 7,
        out_specs=pl.BlockSpec(memory_space=pltpu.VMEM),
        scratch_shapes=scratch,
        compiler_params=pltpu.CompilerParams(
            collective_id=0, has_side_effects=True, vmem_limit_bytes=56 * 1024 * 1024
        ),
        cost_estimate=pl.CostEstimate(
            flops=2 * ROWS * FEAT * (3072 + 2 * BLOCK + 2 * HD),
            bytes_accessed=11_000_000,
            transcendentals=ROWS * FEAT * 4,
        ),
    )(queries, keys, values, log_decay.T, gate, norm_gain.reshape(HEADS, HD), w_out)


def solution(mesh):
    placed = (
        P("seq", "head"),
        P("seq", "head"),
        P("seq", "head"),
        P("seq", "head"),
        P("seq", "head"),
        P("head"),
        P("head", None),
    )
    return jax.shard_map(
        per_device, mesh=mesh, in_specs=placed, out_specs=P("seq", "head"), check_vma=False
    )
```

```python
import jax
import jax.numpy as jnp
from jax import lax
from jax.experimental import pallas as pl
from jax.experimental.pallas import tpu as pltpu
from jax.sharding import PartitionSpec as P

HD = 128
BLOCK = 256
NX, NY, NZ = 4, 4, 8
ROWS = 512
HEADS = 8
FEAT = HEADS * HD
CW = 384
TILE = 128
NT = ROWS // TILE
PARTS = 2
PD = HD // PARTS
FAR_FIRST = (4, 5, 3, 6, 2, 7, 1)
HALF = TILE // 2
EARLY = 8

F32, BF16 = jnp.float32, jnp.bfloat16
EXACT = lax.Precision.HIGHEST
MESH = pl.DeviceIdType.MESH


def remote(src, dst, send_sem, recv_sem, device_id):
    return pltpu.make_async_remote_copy(
        src_ref=src,
        dst_ref=dst,
        send_sem=send_sem,
        recv_sem=recv_sem,
        device_id=device_id,
        device_id_type=MESH,
    )


def columns(index, width=HD):
    return pl.ds(pl.multiple_of(index * width, HD), width)


def kernel(
    q_hbm, k_hbm, v_hbm, ld_hbm, gate_hbm, gain_hbm, w_hbm,
    out,
    q, k, v, ld, gate, gain, w_own, w_peer,
    cb, cumr, att, qs, gg, h_own, h_peer,
    s_end, s_first, s_in, w_pre, cl_pre, t_out, t_in, rows_before, p_out, p_in,
    opp, side, held, fwd, mine, passing, fin,
    load_sem, s1, r1, t_s, t_r, s3, r3, w_s, w_r, h_s, h_r,
    m1_s, m1_r, m2_s, m2_r, m3_s, m3_r, ready_y, ready_x, ready_core,
):
    head, seq = lax.axis_index("head"), lax.axis_index("seq")
    z, y = lax.rem(seq, NZ), lax.div(seq, NZ)
    row0 = seq - z
    core, x = lax.rem(head, 2), lax.div(head, 2)
    other = {"head": head + 1 - 2 * core}
    x_right, x_left, x_opp = lax.rem(x + 1, NX), lax.rem(x + 3, NX), lax.rem(x + 2, NX)
    right, left = {"head": x_right * 2 + core}, {"head": x_left * 2 + core}

    def along_z(off):
        return lax.rem(z + off, NZ)

    def along_y(off):
        return lax.rem(y + off, NY)

    def load(i, src, dst):
        return pltpu.make_async_copy(src, dst, load_sem.at[i])

    ld_load = load(0, ld_hbm, ld)
    kv_loads = [load(1, k_hbm, k), load(2, v_hbm, v)]
    later_loads = [
        load(3, q_hbm, q),
        load(4, gate_hbm, gate),
        load(5, gain_hbm, gain),
    ]
    w_loads = [
        pltpu.make_async_copy(
            w_hbm.at[:, pl.ds(pl.multiple_of((2 * i + core) * CW, HD), CW)],
            w_own.at[i],
            load_sem.at[6 + i],
        )
        for i in range(NX)
    ]
    w_sends = [
        remote(
            w_hbm.at[:, pl.ds(pl.multiple_of((2 * i + 1 - core) * CW, HD), CW)],
            w_peer.at[i],
            w_s.at[i],
            w_r.at[i],
            other,
        )
        for i in range(NX)
    ]

    barrier = pltpu.get_barrier_semaphore()

    def greet(device):
        pl.semaphore_signal(barrier, inc=1, device_id=device, device_id_type=MESH)

    def answer(sem, device):
        pl.semaphore_signal(sem, inc=1, device_id=device, device_id_type=MESH)

    for off in FAR_FIRST:
        greet({"seq": row0 + along_z(off)})
    ld_load.start()
    for copy in kv_loads:
        copy.start()
    for there in range(1, NY):

        @pl.when(there > y)
        def _():
            greet({"seq": there * NZ + z})

    @pl.when(x_right > x)
    def _():
        greet(right)

    @pl.when(x_left > x)
    def _():
        greet(left)

    @pl.when(core == 0)
    def _():
        greet(other)

    greeted = NZ - 1 + y + core + jnp.where(x_right < x, 1, 0) + jnp.where(x_left < x, 1, 0)

    at_row = lax.broadcasted_iota(jnp.int32, (BLOCK, BLOCK), 0)
    at_col = lax.broadcasted_iota(jnp.int32, (BLOCK, BLOCK), 1)
    lower = jnp.where(at_row >= at_col, 1.0, 0.0).astype(F32)
    upper = jnp.where(at_row <= at_col, 1.0, 0.0).astype(F32)
    ld_load.wait()
    for b in range(2):
        rows = slice(b * BLOCK, (b + 1) * BLOCK)
        decay = ld[:, rows]
        cum = lax.dot_general(
            lower, decay, (((1,), (1,)), ((), ())), precision=EXACT, preferred_element_type=F32
        )
        cumr[:, rows] = jnp.dot(decay, upper, precision=EXACT, preferred_element_type=F32)
        for h in range(HEADS):
            cb[rows, h * HD : (h + 1) * HD] = jnp.broadcast_to(cum[:, h : h + 1], (BLOCK, HD))

    def rows_of(part):
        return PD + 16 if part == 0 else PD

    row_at = lax.broadcasted_iota(jnp.int32, (16, HD), 0)

    def split_rows(log):
        high = log.astype(BF16).astype(F32)
        middle = (log - high).astype(BF16).astype(F32)
        low = log - high - middle
        return jnp.where(
            row_at == 0,
            high,
            jnp.where(row_at == 1, middle, jnp.where(row_at == 2, low, 0.0)),
        ).astype(BF16)

    def joined_rows(split):
        wide = split.astype(F32)
        return wide[0:1] + wide[1:2] + wide[2:3]

    def state_copy(part, h):
        return remote(
            s_end.at[part, h, 0 : rows_of(part)],
            s_in.at[part, z, 0 : rows_of(part)],
            s1.at[part, h],
            r1.at[part, z],
            {"seq": row0 + h},
        )

    for copy in kv_loads:
        copy.wait()
    for h in range(HEADS):
        hc = slice(h * HD, (h + 1) * HD)
        ends = []
        for b in range(2):
            rows = slice(b * BLOCK, (b + 1) * BLOCK)
            total = cb[(b + 1) * BLOCK - 1 : (b + 1) * BLOCK, hc]
            weighted = (k[rows, hc].astype(F32) * jnp.exp(total - cb[rows, hc])).astype(BF16)
            ends.append(
                lax.dot_general(
                    weighted, v[rows, hc], (((0,), (0,)), ((), ())), preferred_element_type=F32
                )
            )
        s_first[h] = ends[0].astype(BF16)
        whole = (jnp.exp(cb[ROWS - 1 : ROWS, hc]) * ends[0] + ends[1]).astype(BF16)
        for part in range(PARTS):
            s_end[part, h, 0:PD] = whole[part * PD : (part + 1) * PD]
        s_end[0, h, PD : PD + 16] = split_rows(cb[BLOCK - 1 : BLOCK, hc] + cb[ROWS - 1 : ROWS, hc])

    pl.semaphore_wait(barrier, greeted)
    for part in range(PARTS):
        for off in FAR_FIRST:
            state_copy(part, along_z(off)).start()
    for part in range(PARTS):
        s_in[part, z] = s_end[part, z]
    for there in range(NY - 1):

        @pl.when(there < y)
        def _():
            answer(ready_y.at[y], {"seq": there * NZ + z})

    @pl.when(x_right < x)
    def _():
        answer(ready_x.at[1], right)

    @pl.when(x_left < x)
    def _():
        answer(ready_x.at[0], left)

    @pl.when(core == 1)
    def _():
        answer(ready_core, other)

    for copy in later_loads:
        copy.start()

    @pl.when(core == 0)
    def _():
        pl.semaphore_wait(ready_core, 1)

    for copy in w_sends:
        copy.start()
    for copy in w_loads:
        copy.start()
    for copy in later_loads:
        copy.wait()

    def within(h):
        hc = columns(h)
        for b in range(2):
            rows = slice(b * BLOCK, (b + 1) * BLOCK)
            query = q[rows, hc]
            scores = lax.dot_general(
                query, k[rows, hc], (((1,), (1,)), ((), ())), preferred_element_type=F32
            )
            col = cb[rows, hc]
            between = jnp.concatenate([col, col], axis=1) - cumr[pl.ds(h, 1), rows]
            weights = jnp.exp(jnp.where(at_row >= at_col, jnp.minimum(between, 0.0), -1e30))
            attended = jnp.dot(
                (scores * weights).astype(BF16), v[rows, hc], preferred_element_type=F32
            )
            scaled = query.astype(F32) * jnp.exp(col)
            if b == 1:
                attended += jnp.dot(
                    scaled.astype(BF16), s_first[h], preferred_element_type=F32
                )
                scaled = query.astype(F32) * jnp.exp(col + cb[BLOCK - 1 : BLOCK, hc])
            qs[rows, hc] = scaled.astype(BF16)
            att[rows, hc] = attended
            gg[rows, hc] = gain[pl.ds(h, 1), :] * jax.nn.sigmoid(gate[rows, hc].astype(F32))

    @pl.loop(0, EARLY)
    def _(h):
        within(h)

    def row_copy(part, there):
        return remote(
            t_out.at[part, 0 : rows_of(part)],
            t_in.at[part, y, 0 : rows_of(part)],
            t_s.at[part, there],
            t_r.at[part, y],
            {"seq": there * NZ + z},
        )

    def prefix_copy(part, there):
        return remote(
            p_out.at[part, there],
            p_in.at[part, z],
            s3.at[part, there],
            r3.at[part, z],
            {"seq": row0 + there},
        )

    def prefix(part, there):
        entering = jnp.exp(cl_pre[there : there + 1, :]) * rows_before[part] + w_pre[part, there]
        p_out[part, there] = entering.astype(BF16)

        @pl.when(there != z)
        def _():
            prefix_copy(part, there).start()

    for part in range(PARTS):
        state = jnp.zeros((PD, HD), F32)
        log = jnp.zeros((1, HD), F32)
        for there in range(NZ):
            w_pre[part, there] = state
            if part == 0:
                cl_pre[there : there + 1, :] = log

            @pl.when(there != z)
            def _():
                remote(
                    s_end.at[part, 0, 0 : rows_of(part)],
                    s_in.at[part, there, 0 : rows_of(part)],
                    s1.at[0, 0],
                    r1.at[part, there],
                    other,
                ).wait_recv()

            step = joined_rows(s_in[0, there, PD : PD + 16])
            state = jnp.exp(step) * state + s_in[part, there, 0:PD].astype(F32)
            log = log + step
        t_out[part, 0:PD] = state.astype(BF16)
        if part == 0:
            t_out[0, PD : PD + 16] = split_rows(log)
        for there in range(1, NY):

            @pl.when(there > y)
            def _():
                if part == 0:
                    pl.semaphore_wait(ready_y.at[there], 1)
                row_copy(part, there).start()

    for part in range(PARTS):
        rows_before[part] = jnp.zeros((PD, HD), F32)
        for there in range(NY - 1):

            @pl.when(there < y)
            def _():
                remote(
                    t_out.at[part, 0 : rows_of(part)],
                    t_in.at[part, there, 0 : rows_of(part)],
                    t_s.at[0, 0],
                    t_r.at[part, there],
                    other,
                ).wait_recv()
                rows_before[part] = jnp.exp(
                    joined_rows(t_in[0, there, PD : PD + 16])
                ) * rows_before[part] + t_in[part, there, 0:PD].astype(F32)

        for there in range(NZ // 2):
            prefix(part, there)
    for there in range(NZ // 2, NZ):
        for part in range(PARTS):
            prefix(part, there)
    for part in range(PARTS):
        p_in[part, z] = p_out[part, z]

    @pl.loop(EARLY, HEADS)
    def _(h):
        within(h)

    for copy in w_loads:
        copy.wait()
    for copy in w_sends:
        copy.wait_recv()
    for off in range(1, NZ):
        there = along_z(off)
        for part in range(PARTS):
            remote(
                p_out.at[0, 0], p_in.at[part, there], s3.at[0, 0], r3.at[part, there], other
            ).wait_recv()

    def tile(t):
        return pl.ds(pl.multiple_of(t * TILE, TILE), TILE)

    def hidden_copy(t):
        return remote(h_own.at[tile(t)], h_peer.at[tile(t)], h_s.at[t], h_r.at[t], other)

    def make_hidden(t):
        rows = tile(t)
        for h in range(HEADS):
            hc = slice(h * HD, (h + 1) * HD)
            entering = jnp.concatenate([p_in[part, h] for part in range(PARTS)], axis=0)
            attended = att[rows, hc] + jnp.dot(
                qs[rows, hc], entering, preferred_element_type=F32
            )
            square = jnp.mean(attended * attended, axis=1, keepdims=True)
            h_own[rows, hc] = (attended * lax.rsqrt(square + 1e-06) * gg[rows, hc]).astype(BF16)
        hidden_copy(t).start()

    def chunk(t, i):
        return jnp.dot(h_own[tile(t), :], w_own[i], preferred_element_type=F32) + jnp.dot(
            h_peer[tile(t), :], w_peer[i], preferred_element_type=F32
        )

    targets = (right, left)
    halves = (slice(0, HALF), slice(HALF, TILE))

    def first_copy(t, way):
        return remote(
            opp.at[t, way], fwd.at[way, t], m1_s.at[way, t], m1_r.at[way, t], targets[way]
        )

    def side_copy(t, way):
        return remote(
            side.at[way, t], fin.at[way, t, 1 - way], m2_s.at[way, t], m2_r.at[way, t], targets[way]
        )

    def passing_copy(t, way):
        return remote(
            passing.at[way, t], fin.at[way, t, way], m3_s.at[way, t], m3_r.at[way, t], targets[way]
        )

    def send_far(t):
        hidden_copy(t).wait_recv()
        far = chunk(t, x_opp).astype(BF16)
        for way in range(2):
            opp[t, way] = far[halves[way]]
            first_copy(t, way).start()

    def send_near(t):
        for way, i in ((1, x_left), (0, x_right)):
            near = chunk(t, i)
            side[way, t] = near[halves[1 - way]].astype(BF16)
            side_copy(t, way).start()
            held[way, t] = near[halves[way]]

    def pass_on(t):
        for way in range(2):
            first_copy(t, way).wait_recv()
            passing[way, t] = (held[way, t] + fwd[way, t].astype(F32)).astype(BF16)
            passing_copy(t, way).start()

    @pl.when(x_right > x)
    def _():
        pl.semaphore_wait(ready_x.at[0], 1)

    @pl.when(x_left > x)
    def _():
        pl.semaphore_wait(ready_x.at[1], 1)

    make_hidden(0)

    @pl.loop(0, NT)
    def _(t):
        @pl.when(t < NT - 1)
        def _():
            make_hidden(t + 1)

        send_far(t)

    @pl.loop(0, NT)
    def _(t):
        send_near(t)

        @pl.when(t > 0)
        def _():
            pass_on(t - 1)

    pass_on(NT - 1)

    @pl.loop(0, NT)
    def _(t):
        mine[t] = chunk(t, x)

    for off in range(1, NZ):
        there = along_z(off)
        for part in range(PARTS):
            state_copy(part, there).wait_send()
            prefix_copy(part, there).wait_send()
    for there in range(1, NY):

        @pl.when(there > y)
        def _():
            for part in range(PARTS):
                row_copy(part, there).wait_send()

    for copy in w_sends:
        copy.wait_send()

    @pl.loop(0, NT)
    def _(t):
        hidden_copy(t).wait_send()
        for way in range(2):
            first_copy(t, way).wait_send()
            side_copy(t, way).wait_send()
            passing_copy(t, way).wait_send()

    @pl.loop(0, NT)
    def _(t):
        for way in range(2):
            side_copy(t, way).wait_recv()
            passing_copy(t, way).wait_recv()
        for half in range(2):
            rows = pl.ds(pl.multiple_of(t * TILE + half * HALF, HALF), HALF)
            out[rows, :] = (
                mine[t, halves[half]]
                + fin[0, t, half].astype(F32)
                + fin[1, t, half].astype(F32)
            ).astype(BF16)


def per_device(queries, keys, values, log_decay, gate, norm_gain, w_out):
    vmem, dma = pltpu.VMEM, pltpu.SemaphoreType.DMA
    scratch = [
        vmem((ROWS, FEAT), BF16),
        vmem((ROWS, FEAT), BF16),
        vmem((ROWS, FEAT), BF16),
        vmem((HEADS, ROWS), F32),
        vmem((ROWS, FEAT), BF16),
        vmem((HEADS, HD), F32),
        vmem((NX, FEAT, CW), BF16),
        vmem((NX, FEAT, CW), BF16),
        vmem((ROWS, FEAT), F32),
        vmem((HEADS, ROWS), F32),
        vmem((ROWS, FEAT), F32),
        vmem((ROWS, FEAT), BF16),
        vmem((ROWS, FEAT), F32),
        vmem((ROWS, FEAT), BF16),
        vmem((ROWS, FEAT), BF16),
        vmem((PARTS, HEADS, PD + 16, HD), BF16),
        vmem((HEADS, HD, HD), BF16),
        vmem((PARTS, NZ, PD + 16, HD), BF16),
        vmem((PARTS, NZ, PD, HD), F32),
        vmem((NZ, HD), F32),
        vmem((PARTS, PD + 16, HD), BF16),
        vmem((PARTS, NY, PD + 16, HD), BF16),
        vmem((PARTS, PD, HD), F32),
        vmem((PARTS, NZ, PD, HD), BF16),
        vmem((PARTS, HEADS, PD, HD), BF16),
        vmem((NT, 2, HALF, CW), BF16),
        vmem((2, NT, HALF, CW), BF16),
        vmem((2, NT, HALF, CW), F32),
        vmem((2, NT, HALF, CW), BF16),
        vmem((NT, TILE, CW), F32),
        vmem((2, NT, HALF, CW), BF16),
        vmem((2, NT, 2, HALF, CW), BF16),
        dma((6 + NX,)),
        dma((PARTS, NZ)), dma((PARTS, NZ)),
        dma((PARTS, NY)), dma((PARTS, NY)),
        dma((PARTS, NZ)), dma((PARTS, NZ)),
        dma((NX,)), dma((NX,)),
        dma((NT,)), dma((NT,)),
        dma((2, NT)), dma((2, NT)),
        dma((2, NT)), dma((2, NT)),
        dma((2, NT)), dma((2, NT)),
        pltpu.SemaphoreType.REGULAR((NY,)),
        pltpu.SemaphoreType.REGULAR((2,)),
        pltpu.SemaphoreType.REGULAR,
    ]
    return pl.pallas_call(
        kernel,
        out_shape=pltpu.VMEM((ROWS, CW), BF16),
        in_specs=[pl.BlockSpec(memory_space=pl.ANY)] * 7,
        out_specs=pl.BlockSpec(memory_space=pltpu.VMEM),
        scratch_shapes=scratch,
        compiler_params=pltpu.CompilerParams(
            collective_id=0, has_side_effects=True, vmem_limit_bytes=56 * 1024 * 1024
        ),
        cost_estimate=pl.CostEstimate(
            flops=2 * ROWS * FEAT * (3072 + 2 * BLOCK + 2 * HD),
            bytes_accessed=11_000_000,
            transcendentals=ROWS * FEAT * 4,
        ),
    )(queries, keys, values, log_decay.T, gate, norm_gain.reshape(HEADS, HD), w_out)


def solution(mesh):
    placed = (
        P("seq", "head"),
        P("seq", "head"),
        P("seq", "head"),
        P("seq", "head"),
        P("seq", "head"),
        P("head"),
        P("head", None),
    )
    return jax.shard_map(
        per_device, mesh=mesh, in_specs=placed, out_specs=P("seq", "head"), check_vma=False
    )
```
